32 devices in a mesh: blk: 16 (over z, y, x), col: 2 (over core).
Axes of the slice: x: 2, y: 2, z: 4, core: 2. Of those that a mesh axis runs over, the one named last changes fastest.
Arguments:
- psi: bfloat16 [32, 384, 384], P('blk', 'col')
- dims: int32 [32], P('blk'), may hold values from 192 to 384, as said below
- pattern: int32 [32, 5], P('blk'), may hold values 0 or 1
- left_env: bfloat16 [32, 4, 384, 384], P('blk', 'col')
- right_env: bfloat16 [4, 384, 384], P('col')
Outputs:
- sigma_first: float32 [32, 384, 384], P('blk', 'col')
- sigma_second: float32 [32, 384, 384], P('blk', 'col')
The draws below stay inside these ranges and needn't reach their ends.
Inputs may be any that keep to these rules, and one draw needn't show every extreme that they name: dims[s] lies between 192 and 384.
All inputs are finite; a program needn't handle non-finite values. No bound on the sum of `pattern` on one device may be relied on, other than what follows from the above.
Results may differ from the reference program's by a relative error of at most 0.022.
Values may be sent and summed in bfloat16 or wider, within the bound.
A program may use at most 64 MiB of HBM per device.

```python
import jax
import jax.numpy as jnp
from jax import lax

BS = 384
W_COL = 2
NOFF = 5
SECTORS = 32
W = 4
N_COL = 2


def row_signs(key):
    bits = jax.random.randint(jax.random.fold_in(key, 5), (SECTORS, BS), 0, 2)
    return (2 * bits - 1).astype(jnp.float32)


def draw_psi(key, part):
    signs = row_signs(key)
    key = jax.random.fold_in(key, 11)
    first = jax.random.fold_in(key, 0)
    sector = jnp.arange(SECTORS, dtype=jnp.float32)
    rise = jnp.exp(0.5 * jnp.log(3.0) * sector / max(SECTORS - 1, 1))
    tilt = jnp.where(signs > 0.0, 2.0, 0.5)[:, :, None]
    base = jax.random.normal(first, (SECTORS, BS, BS), jnp.float32)
    return (base * rise[:, None, None] * tilt).astype(jnp.bfloat16)


def draw_dims(key, part):
    key = jax.random.fold_in(key, 23)
    first, second, third = jax.random.split(key, 3)
    values = jax.random.randint(first, (SECTORS,), BS // 2, BS + 1)
    top_at = jax.random.randint(second, (), 0, SECTORS)
    step = jax.random.randint(third, (), 1, SECTORS)
    low_at = (top_at + step) % SECTORS
    values = values.at[top_at].set(BS)
    values = values.at[low_at].set(BS // 2)
    return values.astype(jnp.int32)


def env_noise(key, shape):
    values = jax.random.normal(key, shape, jnp.float32)
    return values / jnp.sqrt(jnp.float32(BS))


def draw_left_env(key, part):
    signs = row_signs(key)
    key = jax.random.fold_in(key, 37)
    noise = env_noise(key, (SECTORS, W, BS, BS))
    sector = jnp.arange(SECTORS, dtype=jnp.float32) / max(SECTORS - 1, 1)
    level = -1.0 + 3.0 * sector
    shift = jnp.float32(W) ** 0.25
    entries = shift * (level[:, None] + 0.5 * signs)
    diag = entries[:, :, None] * jnp.eye(BS, dtype=jnp.float32)[None, :, :]
    noise = noise.at[:, 0].add(diag)
    return noise.astype(jnp.bfloat16)


def draw_right_env(key, part):
    key = jax.random.fold_in(key, 41)
    noise = env_noise(key, (W, BS, BS))
    shift = jnp.float32(W) ** 0.25
    noise = noise.at[0].add(shift * jnp.eye(BS, dtype=jnp.float32))
    return noise.astype(jnp.bfloat16)


def with_ends(array, own_key, smallest, high):
    longest = array.shape.index(max(array.shape))
    spots = []
    for shift in (0, 1):
        where = [jax.random.randint(jax.random.fold_in(own_key, axis), (), 0, length) for axis, length in enumerate(array.shape)]
        where[longest] = (where[longest] + shift) % array.shape[longest]
        spots.append(tuple(where))
    return array.at[spots[0]].set(smallest).at[spots[1]].set(high)


def setup_inputs(seed: int = 0) -> dict:
    streams_of = jax.random.split(jax.random.key(seed), 6)
    psi = draw_psi(jax.random.fold_in(streams_of[5], 71), 0)
    dims = draw_dims(jax.random.fold_in(streams_of[5], 71), 0)
    pattern = with_ends((jax.random.randint(streams_of[2], (SECTORS, NOFF), 0, 4) < 3).astype(jnp.int32), jax.random.fold_in(streams_of[2], 1), 0, 1)
    left_env = draw_left_env(jax.random.fold_in(streams_of[5], 71), 0)
    right_env = draw_right_env(jax.random.fold_in(streams_of[5], 71), 0)
    return dict(psi=psi, dims=dims, pattern=pattern, left_env=left_env, right_env=right_env)


def block_mask(dims):
    index = jnp.arange(BS)
    inside = index[None, :] < dims[:, None]
    return inside[:, :, None] & inside[:, None, :]

def combine_blocks(vector, pattern):
    padded = jnp.pad(vector.astype(jnp.float32), ((2, 2), (0, 0), (0, 0)))
    coeff = pattern.astype(jnp.float32)
    total = jnp.zeros(vector.shape, jnp.float32)
    for offset in range(NOFF):
        total = total + coeff[:, offset, None, None] * padded[offset:offset + SECTORS]
    return total.astype(jnp.bfloat16)

def apply_hamiltonian(vector, pattern, left_env, right_env, mask):
    combined = combine_blocks(vector, pattern)
    right_groups = right_env.astype(jnp.float32).reshape(N_COL, W_COL, BS, BS)

    def one_sector(inputs):
        left_block, z_block = inputs
        temp = jnp.einsum('wab,bc->wac', left_block.astype(jnp.float32), z_block.astype(jnp.float32)).astype(jnp.bfloat16)
        temp = temp.astype(jnp.float32).reshape(N_COL, W_COL, BS, BS)
        parts = jnp.einsum('gwac,gwdc->gad', temp, right_groups)
        parts = lax.optimization_barrier(parts.astype(jnp.bfloat16))
        return lax.optimization_barrier(jnp.sum(parts.astype(jnp.float32), axis=0))
    summed = lax.map(one_sector, (left_env, combined))
    return jnp.where(mask, summed / jnp.sqrt(jnp.float32(W)), jnp.float32(0.0))

def reference(psi, dims, pattern, left_env, right_env):
    mask = block_mask(dims)
    psi_m = jnp.where(mask, psi, jnp.zeros_like(psi))
    sigma_first = apply_hamiltonian(psi_m, pattern, left_env, right_env, mask)
    psi_float = psi_m.astype(jnp.float32)
    theta = jnp.sum(psi_float * sigma_first) / jnp.sum(psi_float * psi_float)
    resid = (sigma_first - theta * psi_float).astype(jnp.bfloat16)
    sigma_second = apply_hamiltonian(resid, pattern, left_env, right_env, mask)
    return (sigma_first, sigma_second)
```

```python
import functools

import jax
import jax.numpy as jnp
from jax import lax
from jax.experimental import pallas as pl
from jax.experimental.pallas import tpu as pltpu
from jax.sharding import PartitionSpec as P

MESH = pl.DeviceIdType.MESH
LANES = 128
HALVES = 2


def kernel(
    n_blk,
    n_col,
    dims,
    pattern,
    psi,
    left_env,
    right_env,
    first_out,
    second_out,
    raw,
    own,
    near,
    far,
    z,
    z_psi,
    left,
    right,
    acc,
    sig,
    stat_own,
    stat_col,
    stat_sum,
    stat_blk,
    local_sem,
    near_send,
    near_recv,
    far_send,
    far_recv,
    z_send,
    z_recv,
    env_send,
    env_recv,
    stat_col_send,
    stat_col_recv,
    stat_blk_send,
    stat_blk_recv,
):
    b = lax.axis_index("blk")
    c = lax.axis_index("col")
    sectors, rows, width = psi.shape
    terms = left_env.shape[1]
    all_terms = terms * n_col
    pieces = width // LANES
    height = rows // HALVES
    chunks = [(p, r) for p in range(pieces) for r in range(HALVES)]
    even = lax.rem(b, 2) == 0
    pair = b + 1 - 2 * lax.rem(b, 2)
    onward = b + 2 - 4 * lax.rem(b, 2)
    source = b - 2 + 4 * lax.rem(b, 2)
    has_onward = (onward >= 0) & (onward < n_blk)
    has_source = (source >= 0) & (source < n_blk)
    my_rows = pl.ds(pl.multiple_of(c * rows, 16), rows)

    load_psi = pltpu.make_async_copy(psi, raw, local_sem.at[0])
    load_psi.start()
    load_left = pltpu.make_async_copy(
        left_env.at[:, :, my_rows, :], left.at[:, pl.ds(c * terms, terms)], local_sem.at[1]
    )
    load_left.start()
    load_right = pltpu.make_async_copy(
        right_env, right.at[pl.ds(c * terms, terms)], local_sem.at[2]
    )
    load_right.start()

    barrier = pltpu.get_barrier_semaphore()

    @pl.loop(1, n_blk)
    def _(i):
        pl.semaphore_signal(
            barrier, inc=1, device_id=(lax.rem(b + i, n_blk), c), device_id_type=MESH
        )

    for k in range(1, n_col):
        pl.semaphore_signal(
            barrier, inc=1, device_id=(b, lax.rem(c + k, n_col)), device_id_type=MESH
        )

    load_psi.wait()
    row_ids = c * rows + lax.broadcasted_iota(jnp.int32, (rows, width), 0)
    col_ids = lax.broadcasted_iota(jnp.int32, (rows, width), 1)
    furthest = jnp.maximum(row_ids, col_ids)
    for s in range(sectors):
        own[0, s] = jnp.where(
            furthest < dims[s], raw[s].astype(jnp.float32), 0.0
        ).astype(jnp.bfloat16)

    @pl.when(jnp.logical_not(has_source))
    def _():
        far[...] = jnp.zeros_like(far)

    pl.semaphore_wait(barrier, n_blk + n_col - 2)

    def cut(ref, h, i):
        p, r = chunks[i]
        return ref.at[h, :, pl.ds(r * height, height), pl.ds(p * LANES, LANES)]

    def to_pair(h, i):
        return pltpu.make_async_remote_copy(
            src_ref=cut(own, h, i),
            dst_ref=cut(near, h, i),
            send_sem=near_send.at[h, i],
            recv_sem=near_recv.at[h, i],
            device_id=(pair, c),
            device_id_type=MESH,
        )

    def to_onward(h, i):
        return pltpu.make_async_remote_copy(
            src_ref=cut(near, h, i),
            dst_ref=cut(far, h, i),
            send_sem=far_send.at[h, i],
            recv_sem=far_recv.at[h, i],
            device_id=(onward, c),
            device_id_type=MESH,
        )

    def z_part(h, i, holder):
        p, r = chunks[i]
        start = pl.multiple_of(holder * rows + r * height, 16)
        return z.at[h, :, pl.ds(start, height), pl.ds(p * LANES, LANES)]

    def z_copy(h, i, k, holder):
        return pltpu.make_async_remote_copy(
            src_ref=z_part(h, i, holder),
            dst_ref=z_part(h, i, holder),
            send_sem=z_send.at[h, k - 1, i],
            recv_sem=z_recv.at[h, k - 1, i],
            device_id=(b, lax.rem(c + k, n_col)),
            device_id_type=MESH,
        )

    def env_copies(k, holder, taker):
        took = pl.ds(pl.multiple_of(taker * rows, 16), rows)
        slot = pl.ds(holder * terms, terms)
        return [
            pltpu.make_async_remote_copy(
                src_ref=src,
                dst_ref=dst,
                send_sem=env_send.at[k - 1, j],
                recv_sem=env_recv.at[k - 1, j],
                device_id=(b, lax.rem(c + k, n_col)),
                device_id_type=MESH,
            )
            for j, (src, dst) in enumerate(
                [
                    (left_env.at[:, :, took, :], left.at[:, slot]),
                    (right_env, right.at[slot]),
                ]
            )
        ]

    def start_halo(h):
        for i in range(len(chunks)):
            to_pair(h, i).start()

    start_halo(0)
    for k in range(1, n_col):
        for copy in env_copies(k, c, lax.rem(c + k, n_col)):
            copy.start()

    coeff = [[pattern[s, j].astype(jnp.float32) for j in range(5)] for s in range(2)]
    zero = jnp.float32(0.0)
    below = ((coeff[0][0], coeff[0][1]), (zero, coeff[1][0]))
    above = ((coeff[0][4], zero), (coeff[1][3], coeff[1][4]))
    inner = ((coeff[0][2], coeff[0][3]), (coeff[1][1], coeff[1][2]))
    near_c = [[jnp.where(even, above[s][k], below[s][k]) for k in range(2)] for s in range(2)]
    far_c = [[jnp.where(even, below[s][k], above[s][k]) for k in range(2)] for s in range(2)]

    def combine(h, i, theta):
        p, r = chunks[i]
        rr, cc = slice(r * height, (r + 1) * height), slice(p * LANES, (p + 1) * LANES)
        start = pl.multiple_of(c * rows + r * height, 16)
        total = [None, None]
        for ref, weights in ((own, inner), (near, near_c), (far, far_c)):
            for k in range(2):
                block = ref[h, k, rr, cc].astype(jnp.float32)
                for s in range(2):
                    term = weights[s][k] * block
                    total[s] = term if total[s] is None else total[s] + term
        for s in range(2):
            if h == 0:
                z_psi[s, rr, cc] = total[s]
            else:
                total[s] = total[s] - theta * z_psi[s, rr, cc]
            z[h, s, pl.ds(start, height), cc] = total[s].astype(jnp.bfloat16)

    def product(h, p):
        cc = slice(p * LANES, (p + 1) * LANES)
        temp = []
        for s in range(2):
            t = jnp.dot(
                left[s].reshape(all_terms * rows, width),
                z[h, s, :, cc],
                preferred_element_type=jnp.float32,
            ).astype(jnp.bfloat16)
            temp.append(t)
        wide = jnp.concatenate(
            [
                jnp.concatenate([t[w * rows : (w + 1) * rows] for t in temp], axis=0)
                for w in range(all_terms)
            ],
            axis=1,
        )
        weights = jnp.concatenate([right[w, :, cc] for w in range(all_terms)], axis=1)
        part = lax.dot_general(
            wide, weights, (((1,), (1,)), ((), ())), preferred_element_type=jnp.float32
        )
        if p == 0:
            acc[...] = part
        else:
            acc[...] += part

    def finish_piece(h, p):
        for r in range(HALVES):
            for k in range(1, n_col):
                z_copy(h, p * HALVES + r, k, lax.rem(c + n_col - k, n_col)).wait_recv()
        if h == 0 and p == 0:
            load_left.wait()
            load_right.wait()
            for k in range(1, n_col):
                for copy in env_copies(k, lax.rem(c + n_col - k, n_col), c):
                    copy.wait_recv()
        product(h, p)

    def apply(h, theta_of):
        theta = None
        count = len(chunks)
        for i in range(count + 2):
            if i < count:
                to_pair(h, i).wait_recv()

                @pl.when(has_onward)
                def _():
                    to_onward(h, i).start()

            j = i - 1
            if 0 <= j < count:

                @pl.when(has_source)
                def _():
                    to_onward(h, j).wait_recv()

                if j == 0 and theta_of is not None:
                    theta = theta_of()
                combine(h, j, theta)
                for k in range(1, n_col):
                    z_copy(h, j, k, c).start()
            j = i - 2
            if j >= 0 and j % HALVES == HALVES - 1:
                finish_piece(h, j // HALVES)

    def masked(s):
        return jnp.where(
            furthest < dims[s],
            acc[s * rows : (s + 1) * rows, :] * (1.0 / float(all_terms) ** 0.5),
            0.0,
        )

    def fold(x):
        x = jnp.sum(x.reshape(rows // 8, 8, width), axis=0)
        out = x[:, :LANES]
        for p in range(1, pieces):
            out = out + x[:, p * LANES : (p + 1) * LANES]
        return out

    apply(0, None)
    for s in range(2):
        sig[0, s] = masked(s)
        own[1, s] = sig[0, s].astype(jnp.bfloat16)
    start_halo(1)
    for q in range(2):
        total = None
        for s in range(2):
            v = own[0, s].astype(jnp.float32)
            term = fold(v * (sig[0, s] if q == 0 else v))
            total = term if total is None else total + term
        stat_own[q] = total

    def stat_to_col(k):
        return pltpu.make_async_remote_copy(
            src_ref=stat_own,
            dst_ref=stat_col.at[k - 1],
            send_sem=stat_col_send.at[k - 1],
            recv_sem=stat_col_recv.at[k - 1],
            device_id=(b, lax.rem(c + k, n_col)),
            device_id_type=MESH,
        )

    def stat_to_blk(i):
        return pltpu.make_async_remote_copy(
            src_ref=stat_sum,
            dst_ref=stat_blk.at[i - 1],
            send_sem=stat_blk_send.at[i - 1],
            recv_sem=stat_blk_recv.at[i - 1],
            device_id=(lax.rem(b + i, n_blk), c),
            device_id_type=MESH,
        )

    for k in range(1, n_col):
        stat_to_col(k).start()
    store_first = pltpu.make_async_copy(sig.at[0], first_out, local_sem.at[3])
    store_first.start()
    for k in range(1, n_col):
        stat_to_col(k).wait_recv()
    total = stat_own[...]
    for k in range(1, n_col):
        total = total + stat_col[k - 1]
    stat_sum[...] = total

    @pl.loop(1, n_blk)
    def _(i):
        stat_to_blk(i).start()

    def theta_of():
        @pl.loop(1, n_blk)
        def _(i):
            stat_to_blk(i).wait_recv()

        total = stat_sum[...] + jnp.sum(stat_blk[...], axis=0)
        sums = [jnp.sum(total[q], axis=(0, 1), keepdims=True) for q in range(2)]
        return sums[0] / sums[1]

    apply(1, theta_of)
    for s in range(2):
        sig[1, s] = masked(s)
    store_second = pltpu.make_async_copy(sig.at[1], second_out, local_sem.at[4])
    store_second.start()

    for h in range(2):
        for i in range(len(chunks)):
            to_pair(h, i).wait_send()
            for k in range(1, n_col):
                z_copy(h, i, k, c).wait_send()

        @pl.when(has_onward)
        def _():
            for i in range(len(chunks)):
                to_onward(h, i).wait_send()

    for k in range(1, n_col):
        for copy in env_copies(k, c, lax.rem(c + k, n_col)):
            copy.wait_send()
        stat_to_col(k).wait_send()

    @pl.loop(1, n_blk)
    def _(i):
        stat_to_blk(i).wait_send()

    store_first.wait()
    store_second.wait()


def body(n_blk, n_col, psi, dims, pattern, left_env, right_env):
    sectors, rows, width = psi.shape
    terms = left_env.shape[1] * n_col
    chunks = (width // LANES) * HALVES
    bf16, f32 = jnp.bfloat16, jnp.float32
    dma = pltpu.SemaphoreType.DMA
    vmem = pltpu.VMEM
    hbm = pl.BlockSpec(memory_space=pl.ANY)
    smem = pl.BlockSpec(memory_space=pltpu.SMEM)
    out = jax.ShapeDtypeStruct(psi.shape, f32)
    return pl.pallas_call(
        functools.partial(kernel, n_blk, n_col),
        out_shape=(out, out),
        in_specs=[smem, smem, hbm, hbm, hbm],
        out_specs=(hbm, hbm),
        scratch_shapes=[
            vmem((sectors, rows, width), bf16),
            vmem((2, sectors, rows, width), bf16),
            vmem((2, sectors, rows, width), bf16),
            vmem((2, sectors, rows, width), bf16),
            vmem((2, sectors, width, width), bf16),
            vmem((sectors, rows, width), f32),
            vmem((sectors, terms, rows, width), bf16),
            vmem((terms, width, width), bf16),
            vmem((sectors * rows, width), f32),
            vmem((2, sectors, rows, width), f32),
            vmem((2, 8, LANES), f32),
            vmem((n_col - 1, 2, 8, LANES), f32),
            vmem((2, 8, LANES), f32),
            vmem((n_blk - 1, 2, 8, LANES), f32),
            dma((5,)),
            dma((2, chunks)),
            dma((2, chunks)),
            dma((2, chunks)),
            dma((2, chunks)),
            dma((2, n_col - 1, chunks)),
            dma((2, n_col - 1, chunks)),
            dma((n_col - 1, 2)),
            dma((n_col - 1, 2)),
            dma((n_col - 1,)),
            dma((n_col - 1,)),
            dma((n_blk - 1,)),
            dma((n_blk - 1,)),
        ],
        compiler_params=pltpu.CompilerParams(
            collective_id=0, has_side_effects=True, vmem_limit_bytes=40 * 1024 * 1024
        ),
    )(dims, pattern, psi, left_env, right_env)


def solution(mesh):
    return jax.shard_map(
        functools.partial(body, mesh.shape["blk"], mesh.shape["col"]),
        mesh=mesh,
        in_specs=(
            P("blk", "col", None),
            P("blk"),
            P("blk", None),
            P("blk", "col", None, None),
            P("col", None, None),
        ),
        out_specs=(P("blk", "col", None), P("blk", "col", None)),
        check_vma=False,
    )
```

```python
import functools

import jax
import jax.numpy as jnp
from jax import lax
from jax.experimental import pallas as pl
from jax.experimental.pallas import tpu as pltpu
from jax.sharding import PartitionSpec as P

MESH = pl.DeviceIdType.MESH
LANES = 128
HALVES = 2


def kernel(
    n_blk,
    n_col,
    dims_in,
    pattern_in,
    psi,
    left_env,
    right_env,
    first_out,
    second_out,
    dims,
    pattern,
    raw,
    own,
    near,
    far,
    z,
    z_psi,
    left,
    right,
    acc,
    sig,
    stat_own,
    stat_col,
    stat_sum,
    stat_blk,
    local_sem,
    store_sem,
    near_send,
    near_recv,
    far_send,
    far_recv,
    z_send,
    z_recv,
    env_send,
    env_recv,
    stat_col_send,
    stat_col_recv,
    stat_blk_send,
    stat_blk_recv,
):
    b = lax.axis_index("blk")
    c = lax.axis_index("col")
    sectors, rows, width = psi.shape
    terms = left_env.shape[1]
    all_terms = terms * n_col
    pieces = width // LANES
    height = rows // HALVES
    chunks = [(p, r) for p in range(pieces) for r in range(HALVES)]
    even = lax.rem(b, 2) == 0
    pair = b + 1 - 2 * lax.rem(b, 2)
    onward = b + 2 - 4 * lax.rem(b, 2)
    source = b - 2 + 4 * lax.rem(b, 2)
    has_onward = (onward >= 0) & (onward < n_blk)
    has_source = (source >= 0) & (source < n_blk)
    my_rows = pl.ds(pl.multiple_of(c * rows, 16), rows)

    load_psi = pltpu.make_async_copy(psi, raw, local_sem.at[0])
    load_psi.start()
    load_dims = pltpu.make_async_copy(dims_in, dims, local_sem.at[3])
    load_dims.start()
    load_pattern = pltpu.make_async_copy(pattern_in, pattern, local_sem.at[4])
    load_pattern.start()
    load_left = pltpu.make_async_copy(
        left_env.at[:, :, my_rows, :], left.at[:, pl.ds(c * terms, terms)], local_sem.at[1]
    )
    load_left.start()
    load_right = pltpu.make_async_copy(
        right_env, right.at[pl.ds(c * terms, terms)], local_sem.at[2]
    )
    load_right.start()

    barrier = pltpu.get_barrier_semaphore()

    @pl.loop(1, n_blk)
    def _(i):
        pl.semaphore_signal(
            barrier, inc=1, device_id=(lax.rem(b + i, n_blk), c), device_id_type=MESH
        )

    for k in range(1, n_col):
        pl.semaphore_signal(
            barrier, inc=1, device_id=(b, lax.rem(c + k, n_col)), device_id_type=MESH
        )

    load_dims.wait()
    load_pattern.wait()
    load_psi.wait()
    row_ids = c * rows + lax.broadcasted_iota(jnp.int32, (rows, width), 0)
    col_ids = lax.broadcasted_iota(jnp.int32, (rows, width), 1)
    furthest = jnp.maximum(row_ids, col_ids)
    for s in range(sectors):
        masked_psi = jnp.where(furthest < dims[s], raw[s].astype(jnp.float32), 0.0)
        for i, (p, r) in enumerate(chunks):
            own[0, i, s] = masked_psi[
                r * height : (r + 1) * height, p * LANES : (p + 1) * LANES
            ].astype(jnp.bfloat16)

    @pl.when(jnp.logical_not(has_source))
    def _():
        far[...] = jnp.zeros_like(far)

    pl.semaphore_wait(barrier, n_blk + n_col - 2)

    def to_pair(h, i):
        return pltpu.make_async_remote_copy(
            src_ref=own.at[h, i],
            dst_ref=near.at[h, i],
            send_sem=near_send.at[h, i],
            recv_sem=near_recv.at[h, i],
            device_id=(pair, c),
            device_id_type=MESH,
        )

    def to_onward(h, i):
        return pltpu.make_async_remote_copy(
            src_ref=near.at[h, i],
            dst_ref=far.at[h, i],
            send_sem=far_send.at[h, i],
            recv_sem=far_recv.at[h, i],
            device_id=(onward, c),
            device_id_type=MESH,
        )

    def z_part(h, i, holder):
        p, r = chunks[i]
        start = pl.multiple_of(holder * rows + r * height, 16)
        return z.at[h, p, :, pl.ds(start, height), :]

    def z_copy(h, i, k, holder):
        return pltpu.make_async_remote_copy(
            src_ref=z_part(h, i, holder),
            dst_ref=z_part(h, i, holder),
            send_sem=z_send.at[h, k - 1, i],
            recv_sem=z_recv.at[h, k - 1, i],
            device_id=(b, lax.rem(c + k, n_col)),
            device_id_type=MESH,
        )

    def env_copies(k, holder, taker):
        took = pl.ds(pl.multiple_of(taker * rows, 16), rows)
        slot = pl.ds(holder * terms, terms)
        return [
            pltpu.make_async_remote_copy(
                src_ref=src,
                dst_ref=dst,
                send_sem=env_send.at[k - 1, j],
                recv_sem=env_recv.at[k - 1, j],
                device_id=(b, lax.rem(c + k, n_col)),
                device_id_type=MESH,
            )
            for j, (src, dst) in enumerate(
                [
                    (left_env.at[:, :, took, :], left.at[:, slot]),
                    (right_env, right.at[slot]),
                ]
            )
        ]

    for i in range(len(chunks)):
        to_pair(0, i).start()
    for k in range(1, n_col):
        for copy in env_copies(k, c, lax.rem(c + k, n_col)):
            copy.start()

    coeff = [[pattern[s, j].astype(jnp.float32) for j in range(5)] for s in range(2)]
    zero = jnp.float32(0.0)
    below = ((coeff[0][0], coeff[0][1]), (zero, coeff[1][0]))
    above = ((coeff[0][4], zero), (coeff[1][3], coeff[1][4]))
    inner = ((coeff[0][2], coeff[0][3]), (coeff[1][1], coeff[1][2]))
    near_c = [[jnp.where(even, above[s][k], below[s][k]) for k in range(2)] for s in range(2)]
    far_c = [[jnp.where(even, below[s][k], above[s][k]) for k in range(2)] for s in range(2)]

    def combine(h, i, theta):
        p, r = chunks[i]
        start = pl.multiple_of(c * rows + r * height, 16)
        total = [None, None]
        for ref, weights in ((own, inner), (near, near_c), (far, far_c)):
            for k in range(2):
                block = ref[h, i, k].astype(jnp.float32)
                for s in range(2):
                    term = weights[s][k] * block
                    total[s] = term if total[s] is None else total[s] + term
        for s in range(2):
            if h == 0:
                z_psi[i, s] = total[s]
            else:
                total[s] = total[s] - theta * z_psi[i, s]
            z[h, p, s, pl.ds(start, height), :] = total[s].astype(jnp.bfloat16)

    def product(h, p):
        cc = slice(p * LANES, (p + 1) * LANES)
        temp = []
        for s in range(2):
            t = jnp.dot(
                left[s].reshape(all_terms * rows, width),
                z[h, p, s],
                preferred_element_type=jnp.float32,
            ).astype(jnp.bfloat16)
            temp.append(t)
        wide = jnp.concatenate(
            [
                jnp.concatenate([t[w * rows : (w + 1) * rows] for t in temp], axis=0)
                for w in range(all_terms)
            ],
            axis=1,
        )
        weights = jnp.concatenate([right[w, :, cc] for w in range(all_terms)], axis=1)
        if p < pieces - 1:
            part = lax.dot_general(
                wide, weights, (((1,), (1,)), ((), ())), preferred_element_type=jnp.float32
            )
            if p == 0:
                acc[...] = part
            else:
                acc[...] += part
            return
        for d in range(pieces):
            dd = slice(d * LANES, (d + 1) * LANES)
            part = lax.dot_general(
                wide, weights[dd], (((1,), (1,)), ((), ())), preferred_element_type=jnp.float32
            )
            part = (part + acc[:, dd]) * (1.0 / float(all_terms) ** 0.5)
            for s in range(2):
                block = jnp.where(
                    furthest[:, dd] < dims[s], part[s * rows : (s + 1) * rows], 0.0
                )
                sig[h, s, :, dd] = block
                if h == 0:
                    for r in range(HALVES):
                        own[1, d * HALVES + r, s] = block[
                            r * height : (r + 1) * height
                        ].astype(jnp.bfloat16)
            if h == 0:
                for r in range(HALVES):
                    to_pair(1, d * HALVES + r).start()
            else:
                store(1, d).start()

    def store(h, d):
        dd = pl.ds(d * LANES, LANES)
        return pltpu.make_async_copy(
            sig.at[h, :, :, dd], (first_out, second_out)[h].at[:, :, dd], store_sem.at[h, d]
        )

    def finish_piece(h, p):
        for r in range(HALVES):
            for k in range(1, n_col):
                z_copy(h, p * HALVES + r, k, lax.rem(c + n_col - k, n_col)).wait_recv()
        if h == 0 and p == 0:
            load_left.wait()
            load_right.wait()
            for k in range(1, n_col):
                for copy in env_copies(k, lax.rem(c + n_col - k, n_col), c):
                    copy.wait_recv()
        product(h, p)

    def apply(h, theta_of, lag):
        theta = None
        count = len(chunks)
        for i in range(count + lag + 1):
            if i < count:
                to_pair(h, i).wait_recv()

                @pl.when(has_onward)
                def _():
                    to_onward(h, i).start()

            j = i - lag
            if 0 <= j < count:

                @pl.when(has_source)
                def _():
                    to_onward(h, j).wait_recv()

                if j == 0 and theta_of is not None:
                    theta = theta_of()
                combine(h, j, theta)
                for k in range(1, n_col):
                    z_copy(h, j, k, c).start()
            j = i - lag - 1
            if j >= 0 and j % HALVES == HALVES - 1:
                finish_piece(h, j // HALVES)

    apply(0, None, 1)
    for q in range(2):
        total = None
        for i, (p, r) in enumerate(chunks):
            for s in range(2):
                v = own[0, i, s].astype(jnp.float32)
                if q == 0:
                    w = sig[0, s, r * height : (r + 1) * height, p * LANES : (p + 1) * LANES]
                else:
                    w = v
                term = jnp.sum((v * w).reshape(height // 8, 8, LANES), axis=0)
                total = term if total is None else total + term
        stat_own[q] = total

    def stat_to_col(k):
        return pltpu.make_async_remote_copy(
            src_ref=stat_own,
            dst_ref=stat_col.at[k - 1],
            send_sem=stat_col_send.at[k - 1],
            recv_sem=stat_col_recv.at[k - 1],
            device_id=(b, lax.rem(c + k, n_col)),
            device_id_type=MESH,
        )

    def stat_to_blk(i):
        return pltpu.make_async_remote_copy(
            src_ref=stat_sum,
            dst_ref=stat_blk.at[i - 1],
            send_sem=stat_blk_send.at[i - 1],
            recv_sem=stat_blk_recv.at[i - 1],
            device_id=(lax.rem(b + i, n_blk), c),
            device_id_type=MESH,
        )

    for k in range(1, n_col):
        stat_to_col(k).start()
    for d in range(pieces):
        store(0, d).start()
    for k in range(1, n_col):
        stat_to_col(k).wait_recv()
    total = stat_own[...]
    for k in range(1, n_col):
        total = total + stat_col[k - 1]
    stat_sum[...] = total

    @pl.loop(1, n_blk)
    def _(i):
        stat_to_blk(i).start()

    def theta_of():
        @pl.loop(1, n_blk)
        def _(i):
            stat_to_blk(i).wait_recv()

        total = stat_sum[...] + jnp.sum(stat_blk[...], axis=0)
        sums = [jnp.sum(total[q], axis=(0, 1), keepdims=True) for q in range(2)]
        return sums[0] / sums[1]

    apply(1, theta_of, 3)

    for h in range(2):
        for i in range(len(chunks)):
            to_pair(h, i).wait_send()
            for k in range(1, n_col):
                z_copy(h, i, k, c).wait_send()

        @pl.when(has_onward)
        def _():
            for i in range(len(chunks)):
                to_onward(h, i).wait_send()

    for k in range(1, n_col):
        for copy in env_copies(k, c, lax.rem(c + k, n_col)):
            copy.wait_send()
        stat_to_col(k).wait_send()

    @pl.loop(1, n_blk)
    def _(i):
        stat_to_blk(i).wait_send()

    for h in range(2):
        for d in range(pieces):
            store(h, d).wait()


def body(n_blk, n_col, psi, dims, pattern, left_env, right_env):
    sectors, rows, width = psi.shape
    terms = left_env.shape[1] * n_col
    chunks = (width // LANES) * HALVES
    halo = (chunks, sectors, rows // HALVES, LANES)
    bf16, f32 = jnp.bfloat16, jnp.float32
    dma = pltpu.SemaphoreType.DMA
    vmem = pltpu.VMEM
    hbm = pl.BlockSpec(memory_space=pl.ANY)
    out = jax.ShapeDtypeStruct(psi.shape, f32)
    return pl.pallas_call(
        functools.partial(kernel, n_blk, n_col),
        out_shape=(out, out),
        in_specs=[hbm] * 5,
        out_specs=(hbm, hbm),
        scratch_shapes=[
            pltpu.SMEM(dims.shape, jnp.int32),
            pltpu.SMEM(pattern.shape, jnp.int32),
            vmem((sectors, rows, width), bf16),
            vmem((2, *halo), bf16),
            vmem((2, *halo), bf16),
            vmem((2, *halo), bf16),
            vmem((2, width // LANES, sectors, width, LANES), bf16),
            vmem(halo, f32),
            vmem((sectors, terms, rows, width), bf16),
            vmem((terms, width, width), bf16),
            vmem((sectors * rows, width), f32),
            vmem((2, sectors, rows, width), f32),
            vmem((2, 8, LANES), f32),
            vmem((n_col - 1, 2, 8, LANES), f32),
            vmem((2, 8, LANES), f32),
            vmem((n_blk - 1, 2, 8, LANES), f32),
            dma((5,)),
            dma((2, width // LANES)),
            dma((2, chunks)),
            dma((2, chunks)),
            dma((2, chunks)),
            dma((2, chunks)),
            dma((2, n_col - 1, chunks)),
            dma((2, n_col - 1, chunks)),
            dma((n_col - 1, 2)),
            dma((n_col - 1, 2)),
            dma((n_col - 1,)),
            dma((n_col - 1,)),
            dma((n_blk - 1,)),
            dma((n_blk - 1,)),
        ],
        compiler_params=pltpu.CompilerParams(
            collective_id=0, has_side_effects=True, vmem_limit_bytes=60 * 1024 * 1024
        ),
    )(dims, pattern, psi, left_env, right_env)


def solution(mesh):
    return jax.shard_map(
        functools.partial(body, mesh.shape["blk"], mesh.shape["col"]),
        mesh=mesh,
        in_specs=(
            P("blk", "col", None),
            P("blk"),
            P("blk", None),
            P("blk", "col", None, None),
            P("col", None, None),
        ),
        out_specs=(P("blk", "col", None), P("blk", "col", None)),
        check_vma=False,
    )
```

```python
import functools

import jax
import jax.numpy as jnp
from jax import lax
from jax.experimental import pallas as pl
from jax.experimental.pallas import tpu as pltpu
from jax.sharding import PartitionSpec as P

MESH = pl.DeviceIdType.MESH
LANES = 128
HALVES = 1


def kernel(
    n_blk,
    n_col,
    dims_in,
    pattern_in,
    psi,
    left_env,
    right_env,
    first_out,
    second_out,
    dims,
    pattern,
    raw,
    own,
    near,
    far,
    z,
    z_psi,
    left,
    right,
    acc,
    sig,
    stat_own,
    stat_col,
    stat_sum,
    stat_blk,
    local_sem,
    store_sem,
    near_send,
    near_recv,
    far_send,
    far_recv,
    z_send,
    z_recv,
    env_send,
    env_recv,
    stat_col_send,
    stat_col_recv,
    stat_blk_send,
    stat_blk_recv,
):
    b = lax.axis_index("blk")
    c = lax.axis_index("col")
    sectors, rows, width = psi.shape
    terms = left_env.shape[1]
    all_terms = terms * n_col
    pieces = width // LANES
    height = rows // HALVES
    chunks = [(p, r) for p in range(pieces) for r in range(HALVES)]
    even = lax.rem(b, 2) == 0
    pair = b + 1 - 2 * lax.rem(b, 2)
    onward = b + 2 - 4 * lax.rem(b, 2)
    source = b - 2 + 4 * lax.rem(b, 2)
    has_onward = (onward >= 0) & (onward < n_blk)
    has_source = (source >= 0) & (source < n_blk)
    my_rows = pl.ds(pl.multiple_of(c * rows, 16), rows)

    load_psi = pltpu.make_async_copy(psi, raw, local_sem.at[0])
    load_psi.start()
    load_dims = pltpu.make_async_copy(dims_in, dims, local_sem.at[3])
    load_dims.start()
    load_pattern = pltpu.make_async_copy(pattern_in, pattern, local_sem.at[4])
    load_pattern.start()
    load_left = pltpu.make_async_copy(
        left_env.at[:, :, my_rows, :], left.at[:, pl.ds(c * terms, terms)], local_sem.at[1]
    )
    load_left.start()
    load_right = pltpu.make_async_copy(
        right_env, right.at[pl.ds(c * terms, terms)], local_sem.at[2]
    )
    load_right.start()

    barrier = pltpu.get_barrier_semaphore()

    @pl.loop(1, n_blk)
    def _(i):
        pl.semaphore_signal(
            barrier, inc=1, device_id=(lax.rem(b + i, n_blk), c), device_id_type=MESH
        )

    for k in range(1, n_col):
        pl.semaphore_signal(
            barrier, inc=1, device_id=(b, lax.rem(c + k, n_col)), device_id_type=MESH
        )

    load_dims.wait()
    load_pattern.wait()
    load_psi.wait()
    row_ids = c * rows + lax.broadcasted_iota(jnp.int32, (rows, width), 0)
    col_ids = lax.broadcasted_iota(jnp.int32, (rows, width), 1)
    furthest = jnp.maximum(row_ids, col_ids)
    for s in range(sectors):
        masked_psi = jnp.where(furthest < dims[s], raw[s].astype(jnp.float32), 0.0)
        for i, (p, r) in enumerate(chunks):
            own[0, i, s] = masked_psi[
                r * height : (r + 1) * height, p * LANES : (p + 1) * LANES
            ].astype(jnp.bfloat16)

    @pl.when(jnp.logical_not(has_source))
    def _():
        far[...] = jnp.zeros_like(far)

    pl.semaphore_wait(barrier, n_blk + n_col - 2)

    def to_pair(h, i):
        return pltpu.make_async_remote_copy(
            src_ref=own.at[h, i],
            dst_ref=near.at[h, i],
            send_sem=near_send.at[h, i],
            recv_sem=near_recv.at[h, i],
            device_id=(pair, c),
            device_id_type=MESH,
        )

    def to_onward(h, i):
        return pltpu.make_async_remote_copy(
            src_ref=near.at[h, i],
            dst_ref=far.at[h, i],
            send_sem=far_send.at[h, i],
            recv_sem=far_recv.at[h, i],
            device_id=(onward, c),
            device_id_type=MESH,
        )

    def z_part(h, i, holder):
        p, r = chunks[i]
        start = pl.multiple_of(holder * rows + r * height, 16)
        return z.at[h, p, :, pl.ds(start, height), :]

    def z_copy(h, i, k, holder):
        return pltpu.make_async_remote_copy(
            src_ref=z_part(h, i, holder),
            dst_ref=z_part(h, i, holder),
            send_sem=z_send.at[h, k - 1, i],
            recv_sem=z_recv.at[h, k - 1, i],
            device_id=(b, lax.rem(c + k, n_col)),
            device_id_type=MESH,
        )

    def env_copies(k, holder, taker):
        took = pl.ds(pl.multiple_of(taker * rows, 16), rows)
        slot = pl.ds(holder * terms, terms)
        return [
            pltpu.make_async_remote_copy(
                src_ref=src,
                dst_ref=dst,
                send_sem=env_send.at[k - 1, j],
                recv_sem=env_recv.at[k - 1, j],
                device_id=(b, lax.rem(c + k, n_col)),
                device_id_type=MESH,
            )
            for j, (src, dst) in enumerate(
                [
                    (left_env.at[:, :, took, :], left.at[:, slot]),
                    (right_env, right.at[slot]),
                ]
            )
        ]

    for i in range(len(chunks)):
        to_pair(0, i).start()
    for k in range(1, n_col):
        for copy in env_copies(k, c, lax.rem(c + k, n_col)):
            copy.start()

    coeff = [[pattern[s, j].astype(jnp.float32) for j in range(5)] for s in range(2)]
    zero = jnp.float32(0.0)
    below = ((coeff[0][0], coeff[0][1]), (zero, coeff[1][0]))
    above = ((coeff[0][4], zero), (coeff[1][3], coeff[1][4]))
    inner = ((coeff[0][2], coeff[0][3]), (coeff[1][1], coeff[1][2]))
    near_c = [[jnp.where(even, above[s][k], below[s][k]) for k in range(2)] for s in range(2)]
    far_c = [[jnp.where(even, below[s][k], above[s][k]) for k in range(2)] for s in range(2)]

    def combine(h, i, theta):
        p, r = chunks[i]
        start = pl.multiple_of(c * rows + r * height, 16)
        total = [None, None]
        for ref, weights in ((own, inner), (near, near_c), (far, far_c)):
            for k in range(2):
                block = ref[h, i, k].astype(jnp.float32)
                for s in range(2):
                    term = weights[s][k] * block
                    total[s] = term if total[s] is None else total[s] + term
        for s in range(2):
            if h == 0:
                z_psi[i, s] = total[s]
            else:
                total[s] = total[s] - theta * z_psi[i, s]
            z[h, p, s, pl.ds(start, height), :] = total[s].astype(jnp.bfloat16)

    def product(h, p):
        cc = slice(p * LANES, (p + 1) * LANES)
        temp = []
        for s in range(2):
            t = jnp.dot(
                left[s].reshape(all_terms * rows, width),
                z[h, p, s],
                preferred_element_type=jnp.float32,
            ).astype(jnp.bfloat16)
            temp.append(t)
        wide = jnp.concatenate(
            [
                jnp.concatenate([t[w * rows : (w + 1) * rows] for t in temp], axis=0)
                for w in range(all_terms)
            ],
            axis=1,
        )
        weights = jnp.concatenate([right[w, :, cc] for w in range(all_terms)], axis=1)
        if p < pieces - 1:
            part = lax.dot_general(
                wide, weights, (((1,), (1,)), ((), ())), preferred_element_type=jnp.float32
            )
            if p == 0:
                acc[...] = part
            else:
                acc[...] += part
            return
        for d in range(pieces):
            dd = slice(d * LANES, (d + 1) * LANES)
            part = lax.dot_general(
                wide, weights[dd], (((1,), (1,)), ((), ())), preferred_element_type=jnp.float32
            )
            part = (part + acc[:, dd]) * (1.0 / float(all_terms) ** 0.5)
            for s in range(2):
                block = jnp.where(
                    furthest[:, dd] < dims[s], part[s * rows : (s + 1) * rows], 0.0
                )
                sig[h, s, :, dd] = block
                if h == 0:
                    for r in range(HALVES):
                        own[1, d * HALVES + r, s] = block[
                            r * height : (r + 1) * height
                        ].astype(jnp.bfloat16)
            if h == 0:
                for r in range(HALVES):
                    to_pair(1, d * HALVES + r).start()
            else:
                store(1, d).start()

    def store(h, d):
        dd = pl.ds(d * LANES, LANES)
        return pltpu.make_async_copy(
            sig.at[h, :, :, dd], (first_out, second_out)[h].at[:, :, dd], store_sem.at[h, d]
        )

    def finish_piece(h, p):
        for r in range(HALVES):
            for k in range(1, n_col):
                z_copy(h, p * HALVES + r, k, lax.rem(c + n_col - k, n_col)).wait_recv()
        if h == 0 and p == 0:
            load_left.wait()
            load_right.wait()
            for k in range(1, n_col):
                for copy in env_copies(k, lax.rem(c + n_col - k, n_col), c):
                    copy.wait_recv()
        product(h, p)

    def apply(h, theta_of, lag):
        theta = None
        count = len(chunks)
        for i in range(count + lag + 1):
            if i < count:
                to_pair(h, i).wait_recv()

                @pl.when(has_onward)
                def _():
                    to_onward(h, i).start()

            j = i - lag
            if 0 <= j < count:

                @pl.when(has_source)
                def _():
                    to_onward(h, j).wait_recv()

                if j == 0 and theta_of is not None:
                    theta = theta_of()
                combine(h, j, theta)
                for k in range(1, n_col):
                    z_copy(h, j, k, c).start()
            j = i - lag - 1
            if j >= 0 and j % HALVES == HALVES - 1:
                finish_piece(h, j // HALVES)

    apply(0, None, 1)
    for q in range(2):
        total = None
        for i, (p, r) in enumerate(chunks):
            for s in range(2):
                v = own[0, i, s].astype(jnp.float32)
                if q == 0:
                    w = sig[0, s, r * height : (r + 1) * height, p * LANES : (p + 1) * LANES]
                else:
                    w = v
                term = jnp.sum((v * w).reshape(height // 8, 8, LANES), axis=0)
                total = term if total is None else total + term
        stat_own[q] = total

    def stat_to_col(k):
        return pltpu.make_async_remote_copy(
            src_ref=stat_own,
            dst_ref=stat_col.at[k - 1],
            send_sem=stat_col_send.at[k - 1],
            recv_sem=stat_col_recv.at[k - 1],
            device_id=(b, lax.rem(c + k, n_col)),
            device_id_type=MESH,
        )

    def stat_to_blk(i):
        return pltpu.make_async_remote_copy(
            src_ref=stat_sum,
            dst_ref=stat_blk.at[i - 1],
            send_sem=stat_blk_send.at[i - 1],
            recv_sem=stat_blk_recv.at[i - 1],
            device_id=(lax.rem(b + i, n_blk), c),
            device_id_type=MESH,
        )

    for k in range(1, n_col):
        stat_to_col(k).start()
    for d in range(pieces):
        store(0, d).start()
    for k in range(1, n_col):
        stat_to_col(k).wait_recv()
    total = stat_own[...]
    for k in range(1, n_col):
        total = total + stat_col[k - 1]
    stat_sum[...] = total

    @pl.loop(1, n_blk)
    def _(i):
        stat_to_blk(i).start()

    def theta_of():
        @pl.loop(1, n_blk)
        def _(i):
            stat_to_blk(i).wait_recv()

        total = stat_sum[...] + jnp.sum(stat_blk[...], axis=0)
        sums = [jnp.sum(total[q], axis=(0, 1), keepdims=True) for q in range(2)]
        return sums[0] / sums[1]

    apply(1, theta_of, 2)

    for h in range(2):
        for i in range(len(chunks)):
            to_pair(h, i).wait_send()
            for k in range(1, n_col):
                z_copy(h, i, k, c).wait_send()

        @pl.when(has_onward)
        def _():
            for i in range(len(chunks)):
                to_onward(h, i).wait_send()

    for k in range(1, n_col):
        for copy in env_copies(k, c, lax.rem(c + k, n_col)):
            copy.wait_send()
        stat_to_col(k).wait_send()

    @pl.loop(1, n_blk)
    def _(i):
        stat_to_blk(i).wait_send()

    for h in range(2):
        for d in range(pieces):
            store(h, d).wait()


def body(n_blk, n_col, psi, dims, pattern, left_env, right_env):
    sectors, rows, width = psi.shape
    terms = left_env.shape[1] * n_col
    chunks = (width // LANES) * HALVES
    halo = (chunks, sectors, rows // HALVES, LANES)
    bf16, f32 = jnp.bfloat16, jnp.float32
    dma = pltpu.SemaphoreType.DMA
    vmem = pltpu.VMEM
    hbm = pl.BlockSpec(memory_space=pl.ANY)
    out = jax.ShapeDtypeStruct(psi.shape, f32)
    return pl.pallas_call(
        functools.partial(kernel, n_blk, n_col),
        out_shape=(out, out),
        in_specs=[hbm] * 5,
        out_specs=(hbm, hbm),
        scratch_shapes=[
            pltpu.SMEM(dims.shape, jnp.int32),
            pltpu.SMEM(pattern.shape, jnp.int32),
            vmem((sectors, rows, width), bf16),
            vmem((2, *halo), bf16),
            vmem((2, *halo), bf16),
            vmem((2, *halo), bf16),
            vmem((2, width // LANES, sectors, width, LANES), bf16),
            vmem(halo, f32),
            vmem((sectors, terms, rows, width), bf16),
            vmem((terms, width, width), bf16),
            vmem((sectors * rows, width), f32),
            vmem((2, sectors, rows, width), f32),
            vmem((2, 8, LANES), f32),
            vmem((n_col - 1, 2, 8, LANES), f32),
            vmem((2, 8, LANES), f32),
            vmem((n_blk - 1, 2, 8, LANES), f32),
            dma((5,)),
            dma((2, width // LANES)),
            dma((2, chunks)),
            dma((2, chunks)),
            dma((2, chunks)),
            dma((2, chunks)),
            dma((2, n_col - 1, chunks)),
            dma((2, n_col - 1, chunks)),
            dma((n_col - 1, 2)),
            dma((n_col - 1, 2)),
            dma((n_col - 1,)),
            dma((n_col - 1,)),
            dma((n_blk - 1,)),
            dma((n_blk - 1,)),
        ],
        compiler_params=pltpu.CompilerParams(
            collective_id=0, has_side_effects=True, vmem_limit_bytes=60 * 1024 * 1024
        ),
    )(dims, pattern, psi, left_env, right_env)


def solution(mesh):
    return jax.shard_map(
        functools.partial(body, mesh.shape["blk"], mesh.shape["col"]),
        mesh=mesh,
        in_specs=(
            P("blk", "col", None),
            P("blk"),
            P("blk", None),
            P("blk", "col", None, None),
            P("col", None, None),
        ),
        out_specs=(P("blk", "col", None), P("blk", "col", None)),
        check_vma=False,
    )
```

```python
import functools

import jax
import jax.numpy as jnp
from jax import lax
from jax.experimental import pallas as pl
from jax.experimental.pallas import tpu as pltpu
from jax.sharding import PartitionSpec as P

MESH = pl.DeviceIdType.MESH
LANES = 128
HALVES = 1
PLANE = 4


def kernel(
    n_blk,
    n_col,
    dims_in,
    pattern_in,
    psi,
    left_env,
    right_env,
    first_out,
    second_out,
    dims,
    pattern,
    raw,
    own,
    near,
    far,
    z,
    z_psi,
    left,
    right,
    acc,
    stat_own,
    stat_mate,
    stat_sum,
    stat_far,
    local_sem,
    near_send,
    near_recv,
    far_send,
    far_recv,
    z_send,
    z_recv,
    env_send,
    env_recv,
    stat_mate_send,
    stat_mate_recv,
    stat_far_send,
    stat_far_recv,
):
    b = lax.axis_index("blk")
    c = lax.axis_index("col")
    sectors, rows, width = psi.shape
    terms = left_env.shape[1]
    all_terms = terms * n_col
    pieces = width // LANES
    height = rows // HALVES
    chunks = [(p, r) for p in range(pieces) for r in range(HALVES)]
    even = lax.rem(b, 2) == 0
    pair = b + 1 - 2 * lax.rem(b, 2)
    onward = b + 2 - 4 * lax.rem(b, 2)
    source = b - 2 + 4 * lax.rem(b, 2)
    has_onward = (onward >= 0) & (onward < n_blk)
    has_source = (source >= 0) & (source < n_blk)
    my_rows = pl.ds(pl.multiple_of(c * rows, 16), rows)

    load_psi = pltpu.make_async_copy(psi, raw, local_sem.at[0])
    load_psi.start()
    load_dims = pltpu.make_async_copy(dims_in, dims, local_sem.at[3])
    load_dims.start()
    load_pattern = pltpu.make_async_copy(pattern_in, pattern, local_sem.at[4])
    load_pattern.start()
    load_left = pltpu.make_async_copy(
        left_env.at[:, :, my_rows, :], left.at[:, pl.ds(c * terms, terms)], local_sem.at[1]
    )
    load_left.start()
    load_right = pltpu.make_async_copy(
        right_env, right.at[pl.ds(c * terms, terms)], local_sem.at[2]
    )
    load_right.start()

    barrier = pltpu.get_barrier_semaphore()

    planes = n_blk // PLANE
    plane, place = b // PLANE, lax.rem(b, PLANE)
    mates = PLANE * n_col

    def mate(m):
        f = lax.rem(place * n_col + c + m, mates)
        return (plane * PLANE + f // n_col, lax.rem(f, n_col))

    def beyond(m):
        return (lax.rem(plane + m, planes) * PLANE + place, c)

    across = jnp.where(place < PLANE // 2, b - 2, b + 2)
    has_across = (across >= 0) & (across < n_blk)

    @pl.when(has_across)
    def _():
        pl.semaphore_signal(barrier, inc=1, device_id=(across, c), device_id_type=MESH)

    @pl.loop(1, planes)
    def _(m):
        pl.semaphore_signal(barrier, inc=1, device_id=beyond(m), device_id_type=MESH)

    @pl.loop(1, mates)
    def _(m):
        pl.semaphore_signal(barrier, inc=1, device_id=mate(m), device_id_type=MESH)

    load_dims.wait()
    load_pattern.wait()
    load_psi.wait()
    row_ids = c * rows + lax.broadcasted_iota(jnp.int32, (rows, width), 0)
    col_ids = lax.broadcasted_iota(jnp.int32, (rows, width), 1)
    furthest = jnp.maximum(row_ids, col_ids)
    for s in range(sectors):
        masked_psi = jnp.where(furthest < dims[s], raw[s].astype(jnp.float32), 0.0)
        for i, (p, r) in enumerate(chunks):
            own[0, i, s] = masked_psi[
                r * height : (r + 1) * height, p * LANES : (p + 1) * LANES
            ].astype(jnp.bfloat16)

    @pl.when(jnp.logical_not(has_source))
    def _():
        far[...] = jnp.zeros_like(far)

    pl.semaphore_wait(barrier, mates + planes - 2 + has_across.astype(jnp.int32))

    def to_pair(h, i):
        return pltpu.make_async_remote_copy(
            src_ref=own.at[h, i],
            dst_ref=near.at[h, i],
            send_sem=near_send.at[h, i],
            recv_sem=near_recv.at[h, i],
            device_id=(pair, c),
            device_id_type=MESH,
        )

    def to_onward(h, i):
        return pltpu.make_async_remote_copy(
            src_ref=near.at[h, i],
            dst_ref=far.at[h, i],
            send_sem=far_send.at[h, i],
            recv_sem=far_recv.at[h, i],
            device_id=(onward, c),
            device_id_type=MESH,
        )

    def z_part(h, i, holder):
        p, r = chunks[i]
        start = pl.multiple_of(holder * rows + r * height, 16)
        return z.at[h, p, :, pl.ds(start, height), :]

    def z_copy(h, i, k, holder):
        return pltpu.make_async_remote_copy(
            src_ref=z_part(h, i, holder),
            dst_ref=z_part(h, i, holder),
            send_sem=z_send.at[h, k - 1, i],
            recv_sem=z_recv.at[h, k - 1, i],
            device_id=(b, lax.rem(c + k, n_col)),
            device_id_type=MESH,
        )

    def env_copies(k, holder, taker):
        took = pl.ds(pl.multiple_of(taker * rows, 16), rows)
        slot = pl.ds(holder * terms, terms)
        return [
            pltpu.make_async_remote_copy(
                src_ref=src,
                dst_ref=dst,
                send_sem=env_send.at[k - 1, j],
                recv_sem=env_recv.at[k - 1, j],
                device_id=(b, lax.rem(c + k, n_col)),
                device_id_type=MESH,
            )
            for j, (src, dst) in enumerate(
                [
                    (left_env.at[:, :, took, :], left.at[:, slot]),
                    (right_env, right.at[slot]),
                ]
            )
        ]

    for i in range(len(chunks)):
        to_pair(0, i).start()
    for k in range(1, n_col):
        for copy in env_copies(k, c, lax.rem(c + k, n_col)):
            copy.start()

    coeff = [[pattern[s, j].astype(jnp.float32) for j in range(5)] for s in range(2)]
    zero = jnp.float32(0.0)
    below = ((coeff[0][0], coeff[0][1]), (zero, coeff[1][0]))
    above = ((coeff[0][4], zero), (coeff[1][3], coeff[1][4]))
    inner = ((coeff[0][2], coeff[0][3]), (coeff[1][1], coeff[1][2]))
    near_c = [[jnp.where(even, above[s][k], below[s][k]) for k in range(2)] for s in range(2)]
    far_c = [[jnp.where(even, below[s][k], above[s][k]) for k in range(2)] for s in range(2)]

    def combine(h, i, theta):
        p, r = chunks[i]
        start = pl.multiple_of(c * rows + r * height, 16)
        total = [None, None]
        for ref, weights in ((own, inner), (near, near_c), (far, far_c)):
            for k in range(2):
                block = ref[h, i, k].astype(jnp.float32)
                for s in range(2):
                    term = weights[s][k] * block
                    total[s] = term if total[s] is None else total[s] + term
        for s in range(2):
            if h == 0:
                z_psi[i, s] = total[s]
            else:
                total[s] = total[s] - theta * z_psi[i, s]
            z[h, p, s, pl.ds(start, height), :] = total[s].astype(jnp.bfloat16)

    def product(h, p):
        cc = slice(p * LANES, (p + 1) * LANES)
        temp = []
        for s in range(2):
            t = jnp.dot(
                left[s].reshape(all_terms * rows, width),
                z[h, p, s],
                preferred_element_type=jnp.float32,
            ).astype(jnp.bfloat16)
            temp.append(t)
        wide = jnp.concatenate(
            [
                jnp.concatenate([t[w * rows : (w + 1) * rows] for t in temp], axis=0)
                for w in range(all_terms)
            ],
            axis=1,
        )
        weights = jnp.concatenate([right[w, :, cc] for w in range(all_terms)], axis=1)
        if p < pieces - 1:
            part = lax.dot_general(
                wide, weights, (((1,), (1,)), ((), ())), preferred_element_type=jnp.float32
            )
            if p == 0:
                acc[...] = part
            else:
                acc[...] += part
            return
        for d in range(pieces):
            dd = slice(d * LANES, (d + 1) * LANES)
            part = lax.dot_general(
                wide, weights[dd], (((1,), (1,)), ((), ())), preferred_element_type=jnp.float32
            )
            part = (part + acc[:, dd]) * (1.0 / float(all_terms) ** 0.5)
            for s in range(2):
                block = jnp.where(
                    furthest[:, dd] < dims[s], part[s * rows : (s + 1) * rows], 0.0
                )
                (first_out, second_out)[h][s, :, dd] = block
                if h == 0:
                    for r in range(HALVES):
                        own[1, d * HALVES + r, s] = block[
                            r * height : (r + 1) * height
                        ].astype(jnp.bfloat16)
            if h == 0:
                for r in range(HALVES):
                    to_pair(1, d * HALVES + r).start()

    def finish_piece(h, p):
        for r in range(HALVES):
            for k in range(1, n_col):
                z_copy(h, p * HALVES + r, k, lax.rem(c + n_col - k, n_col)).wait_recv()
        if h == 0 and p == 0:
            load_left.wait()
            load_right.wait()
            for k in range(1, n_col):
                for copy in env_copies(k, lax.rem(c + n_col - k, n_col), c):
                    copy.wait_recv()
        product(h, p)

    def apply(h, theta_of, lag):
        theta = None
        count = len(chunks)
        for i in range(count + lag + 1):
            if i < count:
                to_pair(h, i).wait_recv()

                @pl.when(has_onward)
                def _():
                    to_onward(h, i).start()

            j = i - lag
            if 0 <= j < count:

                @pl.when(has_source)
                def _():
                    to_onward(h, j).wait_recv()

                if j == 0 and theta_of is not None:
                    theta = theta_of()
                combine(h, j, theta)
                for k in range(1, n_col):
                    z_copy(h, j, k, c).start()
            j = i - lag - 1
            if j >= 0 and j % HALVES == HALVES - 1:
                finish_piece(h, j // HALVES)

    apply(0, None, 1)
    for q in range(2):
        total = None
        for i, (p, r) in enumerate(chunks):
            for s in range(2):
                v = own[0, i, s].astype(jnp.float32)
                if q == 0:
                    w = first_out[s, r * height : (r + 1) * height, p * LANES : (p + 1) * LANES]
                else:
                    w = v
                term = jnp.sum((v * w).reshape(height // 8, 8, LANES), axis=0)
                total = term if total is None else total + term
        stat_own[q] = total

    def stat_to_mate(m):
        return pltpu.make_async_remote_copy(
            src_ref=stat_own,
            dst_ref=stat_mate.at[m - 1],
            send_sem=stat_mate_send.at[m - 1],
            recv_sem=stat_mate_recv.at[m - 1],
            device_id=mate(m),
            device_id_type=MESH,
        )

    def stat_beyond(m):
        return pltpu.make_async_remote_copy(
            src_ref=stat_sum,
            dst_ref=stat_far.at[m - 1],
            send_sem=stat_far_send.at[m - 1],
            recv_sem=stat_far_recv.at[m - 1],
            device_id=beyond(m),
            device_id_type=MESH,
        )

    @pl.loop(1, mates)
    def _(m):
        stat_to_mate(m).start()

    @pl.loop(1, mates)
    def _(m):
        stat_to_mate(m).wait_recv()

    stat_sum[...] = stat_own[...] + jnp.sum(stat_mate[...], axis=0)

    @pl.loop(1, planes)
    def _(m):
        stat_beyond(m).start()

    def theta_of():
        @pl.loop(1, planes)
        def _(m):
            stat_beyond(m).wait_recv()

        total = stat_sum[...] + jnp.sum(stat_far[...], axis=0)
        sums = [jnp.sum(total[q], axis=(0, 1), keepdims=True) for q in range(2)]
        return sums[0] / sums[1]

    apply(1, theta_of, 2)

    for h in range(2):
        for i in range(len(chunks)):
            to_pair(h, i).wait_send()
            for k in range(1, n_col):
                z_copy(h, i, k, c).wait_send()

        @pl.when(has_onward)
        def _():
            for i in range(len(chunks)):
                to_onward(h, i).wait_send()

    for k in range(1, n_col):
        for copy in env_copies(k, c, lax.rem(c + k, n_col)):
            copy.wait_send()

    @pl.loop(1, mates)
    def _(m):
        stat_to_mate(m).wait_send()

    @pl.loop(1, planes)
    def _(m):
        stat_beyond(m).wait_send()


def body(n_blk, n_col, psi, dims, pattern, left_env, right_env):
    sectors, rows, width = psi.shape
    terms = left_env.shape[1] * n_col
    chunks = (width // LANES) * HALVES
    halo = (chunks, sectors, rows // HALVES, LANES)
    mates, planes = PLANE * n_col, n_blk // PLANE
    bf16, f32 = jnp.bfloat16, jnp.float32
    dma = pltpu.SemaphoreType.DMA
    vmem = pltpu.VMEM
    hbm = pl.BlockSpec(memory_space=pl.ANY)
    out = vmem(psi.shape, f32)
    return pl.pallas_call(
        functools.partial(kernel, n_blk, n_col),
        out_shape=(out, out),
        in_specs=[hbm] * 5,
        out_specs=(pl.BlockSpec(memory_space=vmem),) * 2,
        scratch_shapes=[
            pltpu.SMEM(dims.shape, jnp.int32),
            pltpu.SMEM(pattern.shape, jnp.int32),
            vmem((sectors, rows, width), bf16),
            vmem((2, *halo), bf16),
            vmem((2, *halo), bf16),
            vmem((2, *halo), bf16),
            vmem((2, width // LANES, sectors, width, LANES), bf16),
            vmem(halo, f32),
            vmem((sectors, terms, rows, width), bf16),
            vmem((terms, width, width), bf16),
            vmem((sectors * rows, width), f32),
            vmem((2, 8, LANES), f32),
            vmem((mates - 1, 2, 8, LANES), f32),
            vmem((2, 8, LANES), f32),
            vmem((planes - 1, 2, 8, LANES), f32),
            dma((5,)),
            dma((2, chunks)),
            dma((2, chunks)),
            dma((2, chunks)),
            dma((2, chunks)),
            dma((2, n_col - 1, chunks)),
            dma((2, n_col - 1, chunks)),
            dma((n_col - 1, 2)),
            dma((n_col - 1, 2)),
            dma((mates - 1,)),
            dma((mates - 1,)),
            dma((planes - 1,)),
            dma((planes - 1,)),
        ],
        compiler_params=pltpu.CompilerParams(
            collective_id=0, has_side_effects=True, vmem_limit_bytes=60 * 1024 * 1024
        ),
    )(dims, pattern, psi, left_env, right_env)


def solution(mesh):
    return jax.shard_map(
        functools.partial(body, mesh.shape["blk"], mesh.shape["col"]),
        mesh=mesh,
        in_specs=(
            P("blk", "col", None),
            P("blk"),
            P("blk", None),
            P("blk", "col", None, None),
            P("col", None, None),
        ),
        out_specs=(P("blk", "col", None), P("blk", "col", None)),
        check_vma=False,
    )
```

```python
import functools

import jax
import jax.numpy as jnp
from jax import lax
from jax.experimental import pallas as pl
from jax.experimental.pallas import tpu as pltpu
from jax.sharding import PartitionSpec as P

MESH = pl.DeviceIdType.MESH
LANES = 128
HALVES = 1


def kernel(
    n_blk,
    n_col,
    dims_in,
    pattern_in,
    psi,
    left_env,
    right_env,
    first_out,
    second_out,
    dims,
    pattern,
    raw,
    own,
    near,
    far,
    z,
    z_psi,
    left,
    right,
    acc,
    stat_own,
    stat_col,
    stat_sum,
    stat_blk,
    local_sem,
    near_send,
    near_recv,
    far_send,
    far_recv,
    z_send,
    z_recv,
    env_send,
    env_recv,
    stat_col_send,
    stat_col_recv,
    stat_blk_send,
    stat_blk_recv,
):
    b = lax.axis_index("blk")
    c = lax.axis_index("col")
    sectors, rows, width = psi.shape
    terms = left_env.shape[1]
    all_terms = terms * n_col
    pieces = width // LANES
    height = rows // HALVES
    chunks = [(p, r) for p in range(pieces) for r in range(HALVES)]
    even = lax.rem(b, 2) == 0
    pair = b + 1 - 2 * lax.rem(b, 2)
    onward = b + 2 - 4 * lax.rem(b, 2)
    source = b - 2 + 4 * lax.rem(b, 2)
    has_onward = (onward >= 0) & (onward < n_blk)
    has_source = (source >= 0) & (source < n_blk)
    my_rows = pl.ds(pl.multiple_of(c * rows, 16), rows)

    load_psi = pltpu.make_async_copy(psi, raw, local_sem.at[0])
    load_psi.start()
    load_dims = pltpu.make_async_copy(dims_in, dims, local_sem.at[3])
    load_dims.start()
    load_pattern = pltpu.make_async_copy(pattern_in, pattern, local_sem.at[4])
    load_pattern.start()
    load_left = pltpu.make_async_copy(
        left_env.at[:, :, my_rows, :], left.at[:, pl.ds(c * terms, terms)], local_sem.at[1]
    )
    load_left.start()
    load_right = pltpu.make_async_copy(
        right_env, right.at[pl.ds(c * terms, terms)], local_sem.at[2]
    )
    load_right.start()

    barrier = pltpu.get_barrier_semaphore()

    @pl.loop(1, n_blk)
    def _(i):
        pl.semaphore_signal(
            barrier, inc=1, device_id=(lax.rem(b + i, n_blk), c), device_id_type=MESH
        )

    for k in range(1, n_col):
        pl.semaphore_signal(
            barrier, inc=1, device_id=(b, lax.rem(c + k, n_col)), device_id_type=MESH
        )

    load_dims.wait()
    load_pattern.wait()
    load_psi.wait()
    row_ids = c * rows + lax.broadcasted_iota(jnp.int32, (rows, width), 0)
    col_ids = lax.broadcasted_iota(jnp.int32, (rows, width), 1)
    furthest = jnp.maximum(row_ids, col_ids)
    for s in range(sectors):
        masked_psi = jnp.where(furthest < dims[s], raw[s].astype(jnp.float32), 0.0)
        for i, (p, r) in enumerate(chunks):
            own[0, i, s] = masked_psi[
                r * height : (r + 1) * height, p * LANES : (p + 1) * LANES
            ].astype(jnp.bfloat16)

    @pl.when(jnp.logical_not(has_source))
    def _():
        far[...] = jnp.zeros_like(far)

    pl.semaphore_wait(barrier, n_blk + n_col - 2)

    def to_pair(h, i):
        return pltpu.make_async_remote_copy(
            src_ref=own.at[h, i],
            dst_ref=near.at[h, i],
            send_sem=near_send.at[h, i],
            recv_sem=near_recv.at[h, i],
            device_id=(pair, c),
            device_id_type=MESH,
        )

    def to_onward(h, i):
        return pltpu.make_async_remote_copy(
            src_ref=near.at[h, i],
            dst_ref=far.at[h, i],
            send_sem=far_send.at[h, i],
            recv_sem=far_recv.at[h, i],
            device_id=(onward, c),
            device_id_type=MESH,
        )

    def z_part(h, i, holder):
        p, r = chunks[i]
        start = pl.multiple_of(holder * rows + r * height, 16)
        return z.at[h, p, :, pl.ds(start, height), :]

    def z_copy(h, i, k, holder):
        return pltpu.make_async_remote_copy(
            src_ref=z_part(h, i, holder),
            dst_ref=z_part(h, i, holder),
            send_sem=z_send.at[h, k - 1, i],
            recv_sem=z_recv.at[h, k - 1, i],
            device_id=(b, lax.rem(c + k, n_col)),
            device_id_type=MESH,
        )

    def env_copies(k, holder, taker):
        took = pl.ds(pl.multiple_of(taker * rows, 16), rows)
        slot = pl.ds(holder * terms, terms)
        return [
            pltpu.make_async_remote_copy(
                src_ref=src,
                dst_ref=dst,
                send_sem=env_send.at[k - 1, j],
                recv_sem=env_recv.at[k - 1, j],
                device_id=(b, lax.rem(c + k, n_col)),
                device_id_type=MESH,
            )
            for j, (src, dst) in enumerate(
                [
                    (left_env.at[:, :, took, :], left.at[:, slot]),
                    (right_env, right.at[slot]),
                ]
            )
        ]

    for i in range(len(chunks)):
        to_pair(0, i).start()
    for k in range(1, n_col):
        for copy in env_copies(k, c, lax.rem(c + k, n_col)):
            copy.start()

    coeff = [[pattern[s, j].astype(jnp.float32) for j in range(5)] for s in range(2)]
    zero = jnp.float32(0.0)
    below = ((coeff[0][0], coeff[0][1]), (zero, coeff[1][0]))
    above = ((coeff[0][4], zero), (coeff[1][3], coeff[1][4]))
    inner = ((coeff[0][2], coeff[0][3]), (coeff[1][1], coeff[1][2]))
    near_c = [[jnp.where(even, above[s][k], below[s][k]) for k in range(2)] for s in range(2)]
    far_c = [[jnp.where(even, below[s][k], above[s][k]) for k in range(2)] for s in range(2)]

    def combine(h, i, theta):
        p, r = chunks[i]
        start = pl.multiple_of(c * rows + r * height, 16)
        total = [None, None]
        for ref, weights in ((own, inner), (near, near_c), (far, far_c)):
            for k in range(2):
                block = ref[h, i, k].astype(jnp.float32)
                for s in range(2):
                    term = weights[s][k] * block
                    total[s] = term if total[s] is None else total[s] + term
        for s in range(2):
            if h == 0:
                z_psi[i, s] = total[s]
            else:
                total[s] = total[s] - theta * z_psi[i, s]
            z[h, p, s, pl.ds(start, height), :] = total[s].astype(jnp.bfloat16)

    def product(h, p):
        cc = slice(p * LANES, (p + 1) * LANES)
        temp = []
        for s in range(2):
            t = jnp.dot(
                left[s].reshape(all_terms * rows, width),
                z[h, p, s],
                preferred_element_type=jnp.float32,
            ).astype(jnp.bfloat16)
            temp.append(t)
        wide = jnp.concatenate(
            [
                jnp.concatenate([t[w * rows : (w + 1) * rows] for t in temp], axis=0)
                for w in range(all_terms)
            ],
            axis=1,
        )
        weights = jnp.concatenate([right[w, :, cc] for w in range(all_terms)], axis=1)
        if p < pieces - 1:
            part = lax.dot_general(
                wide, weights, (((1,), (1,)), ((), ())), preferred_element_type=jnp.float32
            )
            if p == 0:
                acc[...] = part
            else:
                acc[...] += part
            return
        for d in range(pieces):
            dd = slice(d * LANES, (d + 1) * LANES)
            part = lax.dot_general(
                wide, weights[dd], (((1,), (1,)), ((), ())), preferred_element_type=jnp.float32
            )
            part = (part + acc[:, dd]) * (1.0 / float(all_terms) ** 0.5)
            for s in range(2):
                block = jnp.where(
                    furthest[:, dd] < dims[s], part[s * rows : (s + 1) * rows], 0.0
                )
                (first_out, second_out)[h][s, :, dd] = block
                if h == 0:
                    for r in range(HALVES):
                        own[1, d * HALVES + r, s] = block[
                            r * height : (r + 1) * height
                        ].astype(jnp.bfloat16)
            if h == 0 and d == 0:
                to_pair(1, 0).start()

    def finish_piece(h, p):
        for r in range(HALVES):
            for k in range(1, n_col):
                z_copy(h, p * HALVES + r, k, lax.rem(c + n_col - k, n_col)).wait_recv()
        if h == 0 and p == 0:
            load_left.wait()
            load_right.wait()
            for k in range(1, n_col):
                for copy in env_copies(k, lax.rem(c + n_col - k, n_col), c):
                    copy.wait_recv()
        product(h, p)

    def apply(h, theta_of, lag):
        theta = None
        count = len(chunks)
        for i in range(count + lag + 1):
            if i < count:
                to_pair(h, i).wait_recv()

                @pl.when(has_onward)
                def _():
                    to_onward(h, i).start()

            j = i - lag
            if 0 <= j < count:

                @pl.when(has_source)
                def _():
                    to_onward(h, j).wait_recv()

                if j == 0 and theta_of is not None:
                    theta = theta_of()
                combine(h, j, theta)
                for k in range(1, n_col):
                    z_copy(h, j, k, c).start()
            j = i - lag - 1
            if j >= 0 and j % HALVES == HALVES - 1:
                finish_piece(h, j // HALVES)

    def inner_product(with_sigma):
        total = None
        for i, (p, r) in enumerate(chunks):
            for s in range(2):
                v = own[0, i, s].astype(jnp.float32)
                w = v
                if with_sigma:
                    w = first_out[
                        s, r * height : (r + 1) * height, p * LANES : (p + 1) * LANES
                    ]
                term = jnp.sum((v * w).reshape(height // 8, 8, LANES), axis=0)
                total = term if total is None else total + term
        return total

    stat_own[1] = inner_product(False)
    apply(0, None, 1)
    stat_own[0] = inner_product(True)

    def stat_to_col(k):
        return pltpu.make_async_remote_copy(
            src_ref=stat_own,
            dst_ref=stat_col.at[k - 1],
            send_sem=stat_col_send.at[k - 1],
            recv_sem=stat_col_recv.at[k - 1],
            device_id=(b, lax.rem(c + k, n_col)),
            device_id_type=MESH,
        )

    def stat_to_blk(i):
        return pltpu.make_async_remote_copy(
            src_ref=stat_sum,
            dst_ref=stat_blk.at[i - 1],
            send_sem=stat_blk_send.at[i - 1],
            recv_sem=stat_blk_recv.at[i - 1],
            device_id=(lax.rem(b + i, n_blk), c),
            device_id_type=MESH,
        )

    for k in range(1, n_col):
        stat_to_col(k).start()
    for k in range(1, n_col):
        stat_to_col(k).wait_recv()
    total = stat_own[...]
    for k in range(1, n_col):
        total = total + stat_col[k - 1]
    stat_sum[...] = total

    @pl.loop(1, n_blk)
    def _(i):
        stat_to_blk(i).start()

    for i in range(1, len(chunks)):
        to_pair(1, i).start()

    def theta_of():
        @pl.loop(1, n_blk)
        def _(i):
            stat_to_blk(i).wait_recv()

        total = stat_sum[...] + jnp.sum(stat_blk[...], axis=0)
        sums = [jnp.sum(total[q], axis=(0, 1), keepdims=True) for q in range(2)]
        return sums[0] / sums[1]

    apply(1, theta_of, 2)

    for h in range(2):
        for i in range(len(chunks)):
            to_pair(h, i).wait_send()
            for k in range(1, n_col):
                z_copy(h, i, k, c).wait_send()

        @pl.when(has_onward)
        def _():
            for i in range(len(chunks)):
                to_onward(h, i).wait_send()

    for k in range(1, n_col):
        for copy in env_copies(k, c, lax.rem(c + k, n_col)):
            copy.wait_send()
        stat_to_col(k).wait_send()

    @pl.loop(1, n_blk)
    def _(i):
        stat_to_blk(i).wait_send()


def body(n_blk, n_col, psi, dims, pattern, left_env, right_env):
    sectors, rows, width = psi.shape
    terms = left_env.shape[1] * n_col
    chunks = (width // LANES) * HALVES
    halo = (chunks, sectors, rows // HALVES, LANES)
    bf16, f32 = jnp.bfloat16, jnp.float32
    dma = pltpu.SemaphoreType.DMA
    vmem = pltpu.VMEM
    hbm = pl.BlockSpec(memory_space=pl.ANY)
    out = vmem(psi.shape, f32)
    return pl.pallas_call(
        functools.partial(kernel, n_blk, n_col),
        out_shape=(out, out),
        in_specs=[hbm] * 5,
        out_specs=(pl.BlockSpec(memory_space=vmem),) * 2,
        scratch_shapes=[
            pltpu.SMEM(dims.shape, jnp.int32),
            pltpu.SMEM(pattern.shape, jnp.int32),
            vmem((sectors, rows, width), bf16),
            vmem((2, *halo), bf16),
            vmem((2, *halo), bf16),
            vmem((2, *halo), bf16),
            vmem((2, width // LANES, sectors, width, LANES), bf16),
            vmem(halo, f32),
            vmem((sectors, terms, rows, width), bf16),
            vmem((terms, width, width), bf16),
            vmem((sectors * rows, width), f32),
            vmem((2, 8, LANES), f32),
            vmem((n_col - 1, 2, 8, LANES), f32),
            vmem((2, 8, LANES), f32),
            vmem((n_blk - 1, 2, 8, LANES), f32),
            dma((5,)),
            dma((2, chunks)),
            dma((2, chunks)),
            dma((2, chunks)),
            dma((2, chunks)),
            dma((2, n_col - 1, chunks)),
            dma((2, n_col - 1, chunks)),
            dma((n_col - 1, 2)),
            dma((n_col - 1, 2)),
            dma((n_col - 1,)),
            dma((n_col - 1,)),
            dma((n_blk - 1,)),
            dma((n_blk - 1,)),
        ],
        compiler_params=pltpu.CompilerParams(
            collective_id=0, has_side_effects=True, vmem_limit_bytes=60 * 1024 * 1024
        ),
    )(dims, pattern, psi, left_env, right_env)


def solution(mesh):
    return jax.shard_map(
        functools.partial(body, mesh.shape["blk"], mesh.shape["col"]),
        mesh=mesh,
        in_specs=(
            P("blk", "col", None),
            P("blk"),
            P("blk", None),
            P("blk", "col", None, None),
            P("col", None, None),
        ),
        out_specs=(P("blk", "col", None), P("blk", "col", None)),
        check_vma=False,
    )
```

```python
import functools

import jax
import jax.numpy as jnp
from jax import lax
from jax.experimental import pallas as pl
from jax.experimental.pallas import tpu as pltpu
from jax.sharding import PartitionSpec as P

MESH = pl.DeviceIdType.MESH
LANES = 128
HALVES = 1


def kernel(
    n_blk,
    n_col,
    dims_in,
    pattern_in,
    psi,
    left_env,
    right_env,
    first_out,
    second_out,
    dims,
    pattern,
    raw,
    own,
    near,
    far,
    z,
    z_psi,
    left,
    right,
    acc,
    stat_own,
    stat_mate,
    stat_sum,
    stat_far,
    local_sem,
    near_send,
    near_recv,
    far_send,
    far_recv,
    z_send,
    z_recv,
    env_send,
    env_recv,
    stat_sem,
):
    b = lax.axis_index("blk")
    c = lax.axis_index("col")
    sectors, rows, width = psi.shape
    terms = left_env.shape[1]
    all_terms = terms * n_col
    pieces = width // LANES
    height = rows // HALVES
    chunks = [(p, r) for p in range(pieces) for r in range(HALVES)]
    even = lax.rem(b, 2) == 0
    pair = b + 1 - 2 * lax.rem(b, 2)
    onward = b + 2 - 4 * lax.rem(b, 2)
    source = b - 2 + 4 * lax.rem(b, 2)
    has_onward = (onward >= 0) & (onward < n_blk)
    has_source = (source >= 0) & (source < n_blk)
    my_rows = pl.ds(pl.multiple_of(c * rows, 16), rows)

    load_psi = pltpu.make_async_copy(psi, raw, local_sem.at[0])
    load_psi.start()
    load_dims = pltpu.make_async_copy(dims_in, dims, local_sem.at[3])
    load_dims.start()
    load_pattern = pltpu.make_async_copy(pattern_in, pattern, local_sem.at[4])
    load_pattern.start()
    load_left = pltpu.make_async_copy(
        left_env.at[:, :, my_rows, :], left.at[:, pl.ds(c * terms, terms)], local_sem.at[1]
    )
    load_left.start()
    load_right = pltpu.make_async_copy(
        right_env, right.at[pl.ds(c * terms, terms)], local_sem.at[2]
    )
    load_right.start()

    barrier = pltpu.get_barrier_semaphore()

    side = lax.rem(b, 2)
    mates, others = 2 * n_col, n_blk // 2

    def mate(m):
        f = lax.rem(side * n_col + c + m, mates)
        return (b - side + f // n_col, lax.rem(f, n_col))

    def other(m):
        return (lax.rem(b + 2 * m, n_blk), c)

    @pl.loop(1, others)
    def _(m):
        pl.semaphore_signal(barrier, inc=1, device_id=other(m), device_id_type=MESH)

    for m in range(1, mates):
        pl.semaphore_signal(barrier, inc=1, device_id=mate(m), device_id_type=MESH)

    load_dims.wait()
    load_pattern.wait()
    load_psi.wait()
    row_ids = c * rows + lax.broadcasted_iota(jnp.int32, (rows, width), 0)
    col_ids = lax.broadcasted_iota(jnp.int32, (rows, width), 1)
    furthest = jnp.maximum(row_ids, col_ids)
    for s in range(sectors):
        masked_psi = jnp.where(furthest < dims[s], raw[s].astype(jnp.float32), 0.0)
        for i, (p, r) in enumerate(chunks):
            own[0, i, s] = masked_psi[
                r * height : (r + 1) * height, p * LANES : (p + 1) * LANES
            ].astype(jnp.bfloat16)

    @pl.when(jnp.logical_not(has_source))
    def _():
        far[...] = jnp.zeros_like(far)

    pl.semaphore_wait(barrier, mates + others - 2)

    def to_pair(h, i):
        return pltpu.make_async_remote_copy(
            src_ref=own.at[h, i],
            dst_ref=near.at[h, i],
            send_sem=near_send,
            recv_sem=near_recv.at[h, i],
            device_id=(pair, c),
            device_id_type=MESH,
        )

    def to_onward(h, i):
        return pltpu.make_async_remote_copy(
            src_ref=near.at[h, i],
            dst_ref=far.at[h, i],
            send_sem=far_send,
            recv_sem=far_recv.at[h, i],
            device_id=(onward, c),
            device_id_type=MESH,
        )

    def z_part(h, i, holder):
        p, r = chunks[i]
        start = pl.multiple_of(holder * rows + r * height, 16)
        return z.at[h, p, :, pl.ds(start, height), :]

    def z_copy(h, i, k, holder):
        return pltpu.make_async_remote_copy(
            src_ref=z_part(h, i, holder),
            dst_ref=z_part(h, i, holder),
            send_sem=z_send.at[k - 1],
            recv_sem=z_recv.at[h, k - 1, i],
            device_id=(b, lax.rem(c + k, n_col)),
            device_id_type=MESH,
        )

    def env_copies(k, holder, taker):
        took = pl.ds(pl.multiple_of(taker * rows, 16), rows)
        slot = pl.ds(holder * terms, terms)
        return [
            pltpu.make_async_remote_copy(
                src_ref=src,
                dst_ref=dst,
                send_sem=env_send.at[k - 1, j],
                recv_sem=env_recv.at[k - 1, j],
                device_id=(b, lax.rem(c + k, n_col)),
                device_id_type=MESH,
            )
            for j, (src, dst) in enumerate(
                [
                    (left_env.at[:, :, took, :], left.at[:, slot]),
                    (right_env, right.at[slot]),
                ]
            )
        ]

    for i in range(len(chunks)):
        to_pair(0, i).start()
    for k in range(1, n_col):
        for copy in env_copies(k, c, lax.rem(c + k, n_col)):
            copy.start()

    coeff = [[pattern[s, j].astype(jnp.float32) for j in range(5)] for s in range(2)]
    zero = jnp.float32(0.0)
    below = ((coeff[0][0], coeff[0][1]), (zero, coeff[1][0]))
    above = ((coeff[0][4], zero), (coeff[1][3], coeff[1][4]))
    inner = ((coeff[0][2], coeff[0][3]), (coeff[1][1], coeff[1][2]))
    near_c = [[jnp.where(even, above[s][k], below[s][k]) for k in range(2)] for s in range(2)]
    far_c = [[jnp.where(even, below[s][k], above[s][k]) for k in range(2)] for s in range(2)]

    def combine(h, i, theta):
        p, r = chunks[i]
        start = pl.multiple_of(c * rows + r * height, 16)
        total = [None, None]
        for ref, weights in ((own, inner), (near, near_c), (far, far_c)):
            for k in range(2):
                block = ref[h, i, k].astype(jnp.float32)
                for s in range(2):
                    term = weights[s][k] * block
                    total[s] = term if total[s] is None else total[s] + term
        for s in range(2):
            if h == 0:
                z_psi[i, s] = total[s]
            else:
                total[s] = total[s] - theta * z_psi[i, s]
            z[h, p, s, pl.ds(start, height), :] = total[s].astype(jnp.bfloat16)

    def product(h, p):
        cc = slice(p * LANES, (p + 1) * LANES)
        temp = []
        for s in range(2):
            t = jnp.dot(
                left[s].reshape(all_terms * rows, width),
                z[h, p, s],
                preferred_element_type=jnp.float32,
            ).astype(jnp.bfloat16)
            temp.append(t)
        wide = jnp.concatenate(
            [
                jnp.concatenate([t[w * rows : (w + 1) * rows] for t in temp], axis=0)
                for w in range(all_terms)
            ],
            axis=1,
        )
        weights = jnp.concatenate([right[w, :, cc] for w in range(all_terms)], axis=1)
        part = lax.dot_general(
            wide, weights, (((1,), (1,)), ((), ())), preferred_element_type=jnp.float32
        )
        if p == 0:
            acc[...] = part
            return
        if p < pieces - 1:
            acc[...] += part
            return
        part = (part + acc[...]) * (1.0 / float(all_terms) ** 0.5)
        for s in range(2):
            block = jnp.where(furthest < dims[s], part[s * rows : (s + 1) * rows], 0.0)
            (first_out, second_out)[h][s] = block
            if h == 0:
                for i, (q, r) in enumerate(chunks):
                    own[1, i, s] = block[
                        r * height : (r + 1) * height, q * LANES : (q + 1) * LANES
                    ].astype(jnp.bfloat16)

    def finish_piece(h, p):
        for r in range(HALVES):
            for k in range(1, n_col):
                z_copy(h, p * HALVES + r, k, lax.rem(c + n_col - k, n_col)).wait_recv()
        if h == 0 and p == 0:
            load_left.wait()
            load_right.wait()
            for k in range(1, n_col):
                for copy in env_copies(k, lax.rem(c + n_col - k, n_col), c):
                    copy.wait_recv()
        product(h, p)

    def apply(h, theta_of, lag):
        theta = None
        count = len(chunks)
        for i in range(count + lag + 1):
            if i < count:
                to_pair(h, i).wait_recv()

                @pl.when(has_onward)
                def _():
                    to_onward(h, i).start()

            j = i - lag
            if 0 <= j < count:

                @pl.when(has_source)
                def _():
                    to_onward(h, j).wait_recv()

                if j == 0 and theta_of is not None:
                    theta = theta_of()
                combine(h, j, theta)
                for k in range(1, n_col):
                    z_copy(h, j, k, c).start()
            j = i - lag - 1
            if j >= 0 and j % HALVES == HALVES - 1:
                finish_piece(h, j // HALVES)

    def settle(ref, sem):
        pltpu.make_async_copy(ref, ref, sem).wait()

    def inner_product(with_sigma):
        total = None
        for i, (p, r) in enumerate(chunks):
            for s in range(2):
                v = own[0, i, s].astype(jnp.float32)
                w = v
                if with_sigma:
                    w = first_out[
                        s, r * height : (r + 1) * height, p * LANES : (p + 1) * LANES
                    ]
                term = jnp.sum((v * w).reshape(height // 8, 8, LANES), axis=0)
                total = term if total is None else total + term
        return total

    stat_own[1] = inner_product(False)
    apply(0, None, 1)
    stat_own[0] = inner_product(True)

    def stat_to_mate(m):
        return pltpu.make_async_remote_copy(
            src_ref=stat_own,
            dst_ref=stat_mate.at[m - 1],
            send_sem=stat_sem.at[0],
            recv_sem=stat_sem.at[1],
            device_id=mate(m),
            device_id_type=MESH,
        )

    def stat_to_other(m):
        return pltpu.make_async_remote_copy(
            src_ref=stat_sum,
            dst_ref=stat_far.at[m - 1],
            send_sem=stat_sem.at[2],
            recv_sem=stat_sem.at[3],
            device_id=other(m),
            device_id_type=MESH,
        )

    for m in range(1, mates):
        stat_to_mate(m).start()
    for i in range(len(chunks)):
        to_pair(1, i).start()
    settle(stat_mate, stat_sem.at[1])
    stat_sum[...] = stat_own[...] + jnp.sum(stat_mate[...], axis=0)

    @pl.loop(1, others)
    def _(m):
        stat_to_other(m).start()

    def theta_of():
        settle(stat_far, stat_sem.at[3])
        total = stat_sum[...] + jnp.sum(stat_far[...], axis=0)
        sums = [jnp.sum(total[q], axis=(0, 1), keepdims=True) for q in range(2)]
        return sums[0] / sums[1]

    apply(1, theta_of, 1)

    settle(stat_mate, stat_sem.at[0])
    settle(stat_far, stat_sem.at[2])
    settle(own, near_send)

    @pl.when(has_onward)
    def _():
        settle(near, far_send)

    for k in range(1, n_col):
        settle(own, z_send.at[k - 1])
        for copy in env_copies(k, c, lax.rem(c + k, n_col)):
            copy.wait_send()


def body(n_blk, n_col, psi, dims, pattern, left_env, right_env):
    sectors, rows, width = psi.shape
    terms = left_env.shape[1] * n_col
    chunks = (width // LANES) * HALVES
    halo = (chunks, sectors, rows // HALVES, LANES)
    bf16, f32 = jnp.bfloat16, jnp.float32
    dma = pltpu.SemaphoreType.DMA
    vmem = pltpu.VMEM
    hbm = pl.BlockSpec(memory_space=pl.ANY)
    out = vmem(psi.shape, f32)
    return pl.pallas_call(
        functools.partial(kernel, n_blk, n_col),
        out_shape=(out, out),
        in_specs=[hbm] * 5,
        out_specs=(pl.BlockSpec(memory_space=vmem),) * 2,
        scratch_shapes=[
            pltpu.SMEM(dims.shape, jnp.int32),
            pltpu.SMEM(pattern.shape, jnp.int32),
            vmem((sectors, rows, width), bf16),
            vmem((2, *halo), bf16),
            vmem((2, *halo), bf16),
            vmem((2, *halo), bf16),
            vmem((2, width // LANES, sectors, width, LANES), bf16),
            vmem(halo, f32),
            vmem((sectors, terms, rows, width), bf16),
            vmem((terms, width, width), bf16),
            vmem((sectors * rows, width), f32),
            vmem((2, 8, LANES), f32),
            vmem((2 * n_col - 1, 2, 8, LANES), f32),
            vmem((2, 8, LANES), f32),
            vmem((n_blk // 2 - 1, 2, 8, LANES), f32),
            dma((5,)),
            dma(()),
            dma((2, chunks)),
            dma(()),
            dma((2, chunks)),
            dma((n_col - 1,)),
            dma((2, n_col - 1, chunks)),
            dma((n_col - 1, 2)),
            dma((n_col - 1, 2)),
            dma((4,)),
        ],
        compiler_params=pltpu.CompilerParams(
            collective_id=0, has_side_effects=True, vmem_limit_bytes=60 * 1024 * 1024
        ),
    )(dims, pattern, psi, left_env, right_env)


def solution(mesh):
    return jax.shard_map(
        functools.partial(body, mesh.shape["blk"], mesh.shape["col"]),
        mesh=mesh,
        in_specs=(
            P("blk", "col", None),
            P("blk"),
            P("blk", None),
            P("blk", "col", None, None),
            P("col", None, None),
        ),
        out_specs=(P("blk", "col", None), P("blk", "col", None)),
        check_vma=False,
    )
```

```python
import functools

import jax
import jax.numpy as jnp
from jax import lax
from jax.experimental import pallas as pl
from jax.experimental.pallas import tpu as pltpu
from jax.sharding import PartitionSpec as P

MESH = pl.DeviceIdType.MESH
LANES = 128
HALVES = 1


def kernel(
    n_blk,
    n_col,
    dims_in,
    pattern_in,
    psi,
    left_env,
    right_env,
    first_out,
    second_out,
    dims,
    pattern,
    raw,
    own,
    near,
    far,
    z,
    z_psi,
    left,
    right,
    turned,
    acc,
    stat_own,
    stat_mate,
    stat_sum,
    stat_far,
    local_sem,
    near_send,
    near_recv,
    far_send,
    far_recv,
    z_send,
    z_recv,
    env_send,
    env_recv,
    stat_sem,
):
    b = lax.axis_index("blk")
    c = lax.axis_index("col")
    sectors, rows, width = psi.shape
    terms = left_env.shape[1]
    all_terms = terms * n_col
    pieces = width // LANES
    height = rows // HALVES
    chunks = [(p, r) for p in range(pieces) for r in range(HALVES)]
    even = lax.rem(b, 2) == 0
    pair = b + 1 - 2 * lax.rem(b, 2)
    onward = b + 2 - 4 * lax.rem(b, 2)
    source = b - 2 + 4 * lax.rem(b, 2)
    has_onward = (onward >= 0) & (onward < n_blk)
    has_source = (source >= 0) & (source < n_blk)
    my_rows = pl.ds(pl.multiple_of(c * rows, 16), rows)

    load_psi = pltpu.make_async_copy(psi, raw, local_sem.at[0])
    load_psi.start()
    load_dims = pltpu.make_async_copy(dims_in, dims, local_sem.at[3])
    load_dims.start()
    load_pattern = pltpu.make_async_copy(pattern_in, pattern, local_sem.at[4])
    load_pattern.start()
    load_left = pltpu.make_async_copy(
        left_env.at[:, :, my_rows, :], left.at[:, pl.ds(c * terms, terms)], local_sem.at[1]
    )
    load_left.start()
    load_right = pltpu.make_async_copy(
        right_env, right.at[pl.ds(c * terms, terms)], local_sem.at[2]
    )
    load_right.start()

    barrier = pltpu.get_barrier_semaphore()

    side = lax.rem(b, 2)
    mates, others = 2 * n_col, n_blk // 2

    def mate(m):
        f = lax.rem(side * n_col + c + m, mates)
        return (b - side + f // n_col, lax.rem(f, n_col))

    def other(m):
        return (lax.rem(b + 2 * m, n_blk), c)

    @pl.loop(1, others)
    def _(m):
        pl.semaphore_signal(barrier, inc=1, device_id=other(m), device_id_type=MESH)

    for m in range(1, mates):
        pl.semaphore_signal(barrier, inc=1, device_id=mate(m), device_id_type=MESH)

    load_dims.wait()
    load_pattern.wait()
    load_psi.wait()
    row_ids = c * rows + lax.broadcasted_iota(jnp.int32, (rows, width), 0)
    col_ids = lax.broadcasted_iota(jnp.int32, (rows, width), 1)
    furthest = jnp.maximum(row_ids, col_ids)
    for s in range(sectors):
        masked_psi = jnp.where(furthest < dims[s], raw[s].astype(jnp.float32), 0.0)
        for i, (p, r) in enumerate(chunks):
            own[0, i, s] = masked_psi[
                r * height : (r + 1) * height, p * LANES : (p + 1) * LANES
            ].astype(jnp.bfloat16)

    @pl.when(jnp.logical_not(has_source))
    def _():
        far[...] = jnp.zeros_like(far)

    pl.semaphore_wait(barrier, mates + others - 2)

    def to_pair(h, i):
        return pltpu.make_async_remote_copy(
            src_ref=own.at[h, i],
            dst_ref=near.at[h, i],
            send_sem=near_send,
            recv_sem=near_recv.at[h, i],
            device_id=(pair, c),
            device_id_type=MESH,
        )

    def to_onward(h, i):
        return pltpu.make_async_remote_copy(
            src_ref=near.at[h, i],
            dst_ref=far.at[h, i],
            send_sem=far_send,
            recv_sem=far_recv.at[h, i],
            device_id=(onward, c),
            device_id_type=MESH,
        )

    def z_part(h, i, holder):
        p, r = chunks[i]
        start = pl.multiple_of(holder * rows + r * height, 16)
        return z.at[h, p, :, pl.ds(start, height), :]

    def z_copy(h, i, k, holder):
        return pltpu.make_async_remote_copy(
            src_ref=z_part(h, i, holder),
            dst_ref=z_part(h, i, holder),
            send_sem=z_send.at[k - 1],
            recv_sem=z_recv.at[h, k - 1, i],
            device_id=(b, lax.rem(c + k, n_col)),
            device_id_type=MESH,
        )

    def env_copies(k, holder, taker):
        took = pl.ds(pl.multiple_of(taker * rows, 16), rows)
        slot = pl.ds(holder * terms, terms)
        return [
            pltpu.make_async_remote_copy(
                src_ref=src,
                dst_ref=dst,
                send_sem=env_send.at[k - 1, j],
                recv_sem=env_recv.at[k - 1, j],
                device_id=(b, lax.rem(c + k, n_col)),
                device_id_type=MESH,
            )
            for j, (src, dst) in enumerate(
                [
                    (left_env.at[:, :, took, :], left.at[:, slot]),
                    (right_env, right.at[slot]),
                ]
            )
        ]

    for i in range(len(chunks)):
        to_pair(0, i).start()
    for k in range(1, n_col):
        for copy in env_copies(k, c, lax.rem(c + k, n_col)):
            copy.start()

    coeff = [[pattern[s, j].astype(jnp.float32) for j in range(5)] for s in range(2)]
    zero = jnp.float32(0.0)
    below = ((coeff[0][0], coeff[0][1]), (zero, coeff[1][0]))
    above = ((coeff[0][4], zero), (coeff[1][3], coeff[1][4]))
    inner = ((coeff[0][2], coeff[0][3]), (coeff[1][1], coeff[1][2]))
    near_c = [[jnp.where(even, above[s][k], below[s][k]) for k in range(2)] for s in range(2)]
    far_c = [[jnp.where(even, below[s][k], above[s][k]) for k in range(2)] for s in range(2)]

    def combine(h, i, theta):
        p, r = chunks[i]
        start = pl.multiple_of(c * rows + r * height, 16)
        total = [None, None]
        for ref, weights in ((own, inner), (near, near_c), (far, far_c)):
            for k in range(2):
                block = ref[h, i, k].astype(jnp.float32)
                for s in range(2):
                    term = weights[s][k] * block
                    total[s] = term if total[s] is None else total[s] + term
        for s in range(2):
            if h == 0:
                z_psi[i, s] = total[s]
            else:
                total[s] = total[s] - theta * z_psi[i, s]
            z[h, p, s, pl.ds(start, height), :] = total[s].astype(jnp.bfloat16)

    def product(h, p):
        temp = []
        for s in range(2):
            t = jnp.dot(
                left[s].reshape(all_terms * rows, width),
                z[h, p, s],
                preferred_element_type=jnp.float32,
            ).astype(jnp.bfloat16)
            temp.append(t)
        wide = jnp.concatenate(
            [
                jnp.concatenate([t[w * rows : (w + 1) * rows] for t in temp], axis=0)
                for w in range(all_terms)
            ],
            axis=1,
        )
        part = jnp.dot(wide, turned[p], preferred_element_type=jnp.float32)
        if p == 0:
            acc[...] = part
            return
        if p < pieces - 1:
            acc[...] += part
            return
        part = (part + acc[...]) * (1.0 / float(all_terms) ** 0.5)
        for s in range(2):
            block = jnp.where(furthest < dims[s], part[s * rows : (s + 1) * rows], 0.0)
            (first_out, second_out)[h][s] = block
            if h == 0:
                for i, (q, r) in enumerate(chunks):
                    own[1, i, s] = block[
                        r * height : (r + 1) * height, q * LANES : (q + 1) * LANES
                    ].astype(jnp.bfloat16)

    def finish_piece(h, p):
        for r in range(HALVES):
            for k in range(1, n_col):
                z_copy(h, p * HALVES + r, k, lax.rem(c + n_col - k, n_col)).wait_recv()
        product(h, p)

    def settle_env():
        load_left.wait()
        load_right.wait()
        for k in range(1, n_col):
            for copy in env_copies(k, lax.rem(c + n_col - k, n_col), c):
                copy.wait_recv()
        for p in range(pieces):
            for w in range(all_terms):
                turned[p, w * LANES : (w + 1) * LANES, :] = right[
                    w, :, p * LANES : (p + 1) * LANES
                ].T

    def apply(h, theta_of, lag):
        theta = None
        count = len(chunks)
        for i in range(count + lag + 1):
            if i < count:
                to_pair(h, i).wait_recv()

                @pl.when(has_onward)
                def _():
                    to_onward(h, i).start()

                if h == 0 and i == 0:
                    settle_env()

            j = i - lag
            if 0 <= j < count:

                @pl.when(has_source)
                def _():
                    to_onward(h, j).wait_recv()

                if j == 0 and theta_of is not None:
                    theta = theta_of()
                combine(h, j, theta)
                for k in range(1, n_col):
                    z_copy(h, j, k, c).start()
            j = i - lag - 1
            if j >= 0 and j % HALVES == HALVES - 1:
                finish_piece(h, j // HALVES)

    def settle(ref, sem):
        pltpu.make_async_copy(ref, ref, sem).wait()

    def inner_product(with_sigma):
        total = None
        for i, (p, r) in enumerate(chunks):
            for s in range(2):
                v = own[0, i, s].astype(jnp.float32)
                w = v
                if with_sigma:
                    w = first_out[
                        s, r * height : (r + 1) * height, p * LANES : (p + 1) * LANES
                    ]
                term = jnp.sum((v * w).reshape(height // 8, 8, LANES), axis=0)
                total = term if total is None else total + term
        return total

    stat_own[1] = inner_product(False)
    apply(0, None, 1)
    stat_own[0] = inner_product(True)

    def stat_to_mate(m):
        return pltpu.make_async_remote_copy(
            src_ref=stat_own,
            dst_ref=stat_mate.at[m - 1],
            send_sem=stat_sem.at[0],
            recv_sem=stat_sem.at[1],
            device_id=mate(m),
            device_id_type=MESH,
        )

    def stat_to_other(m):
        return pltpu.make_async_remote_copy(
            src_ref=stat_sum,
            dst_ref=stat_far.at[m - 1],
            send_sem=stat_sem.at[2],
            recv_sem=stat_sem.at[3],
            device_id=other(m),
            device_id_type=MESH,
        )

    for m in range(1, mates):
        stat_to_mate(m).start()
    for i in range(len(chunks)):
        to_pair(1, i).start()
    settle(stat_mate, stat_sem.at[1])
    stat_sum[...] = stat_own[...] + jnp.sum(stat_mate[...], axis=0)

    @pl.loop(1, others)
    def _(m):
        stat_to_other(m).start()

    def theta_of():
        settle(stat_far, stat_sem.at[3])
        total = stat_sum[...] + jnp.sum(stat_far[...], axis=0)
        sums = [jnp.sum(total[q], axis=(0, 1), keepdims=True) for q in range(2)]
        return sums[0] / sums[1]

    apply(1, theta_of, 1)

    settle(stat_mate, stat_sem.at[0])
    settle(stat_far, stat_sem.at[2])
    settle(own, near_send)

    @pl.when(has_onward)
    def _():
        settle(near, far_send)

    for k in range(1, n_col):
        settle(own, z_send.at[k - 1])
        for copy in env_copies(k, c, lax.rem(c + k, n_col)):
            copy.wait_send()


def write_out(first, second, first_out, second_out, sem):
    copies = [
        pltpu.make_async_copy(first, first_out, sem.at[0]),
        pltpu.make_async_copy(second, second_out, sem.at[1]),
    ]
    for copy in copies:
        copy.start()
    for copy in copies:
        copy.wait()


def body(n_blk, n_col, psi, dims, pattern, left_env, right_env):
    sectors, rows, width = psi.shape
    terms = left_env.shape[1] * n_col
    chunks = (width // LANES) * HALVES
    halo = (chunks, sectors, rows // HALVES, LANES)
    bf16, f32 = jnp.bfloat16, jnp.float32
    dma = pltpu.SemaphoreType.DMA
    vmem = pltpu.VMEM
    hbm = pl.BlockSpec(memory_space=pl.ANY)
    out = vmem(psi.shape, f32)
    first, second = pl.pallas_call(
        functools.partial(kernel, n_blk, n_col),
        out_shape=(out, out),
        in_specs=[hbm] * 5,
        out_specs=(pl.BlockSpec(memory_space=vmem),) * 2,
        scratch_shapes=[
            pltpu.SMEM(dims.shape, jnp.int32),
            pltpu.SMEM(pattern.shape, jnp.int32),
            vmem((sectors, rows, width), bf16),
            vmem((2, *halo), bf16),
            vmem((2, *halo), bf16),
            vmem((2, *halo), bf16),
            vmem((2, width // LANES, sectors, width, LANES), bf16),
            vmem(halo, f32),
            vmem((sectors, terms, rows, width), bf16),
            vmem((terms, width, width), bf16),
            vmem((width // LANES, terms * LANES, width), bf16),
            vmem((sectors * rows, width), f32),
            vmem((2, 8, LANES), f32),
            vmem((2 * n_col - 1, 2, 8, LANES), f32),
            vmem((2, 8, LANES), f32),
            vmem((n_blk // 2 - 1, 2, 8, LANES), f32),
            dma((5,)),
            dma(()),
            dma((2, chunks)),
            dma(()),
            dma((2, chunks)),
            dma((n_col - 1,)),
            dma((2, n_col - 1, chunks)),
            dma((n_col - 1, 2)),
            dma((n_col - 1, 2)),
            dma((4,)),
        ],
        compiler_params=pltpu.CompilerParams(
            collective_id=0, has_side_effects=True, vmem_limit_bytes=60 * 1024 * 1024
        ),
    )(dims, pattern, psi, left_env, right_env)
    out = jax.ShapeDtypeStruct(psi.shape, f32)
    return pl.pallas_call(
        write_out,
        out_shape=(out, out),
        in_specs=[pl.BlockSpec(memory_space=vmem)] * 2,
        out_specs=(hbm, hbm),
        scratch_shapes=[dma((2,))],
    )(first, second)


def solution(mesh):
    return jax.shard_map(
        functools.partial(body, mesh.shape["blk"], mesh.shape["col"]),
        mesh=mesh,
        in_specs=(
            P("blk", "col", None),
            P("blk"),
            P("blk", None),
            P("blk", "col", None, None),
            P("col", None, None),
        ),
        out_specs=(P("blk", "col", None), P("blk", "col", None)),
        check_vma=False,
    )
```

```python
import functools

import jax
import jax.numpy as jnp
from jax import lax
from jax.experimental import pallas as pl
from jax.experimental.pallas import tpu as pltpu
from jax.sharding import PartitionSpec as P

MESH = pl.DeviceIdType.MESH
LANES = 128
HALVES = 1


def kernel(
    n_blk,
    n_col,
    dims_in,
    pattern_in,
    psi,
    left_env,
    right_env,
    first_out,
    second_out,
    dims,
    pattern,
    raw,
    own,
    near,
    far,
    z,
    z_psi,
    left,
    right,
    turned,
    acc,
    stat_own,
    stat_mate,
    stat_sum,
    stat_far,
    local_sem,
    near_send,
    near_recv,
    far_send,
    far_recv,
    direct_send,
    direct_recv,
    z_send,
    z_recv,
    env_send,
    env_recv,
    stat_sem,
):
    b = lax.axis_index("blk")
    c = lax.axis_index("col")
    sectors, rows, width = psi.shape
    terms = left_env.shape[1]
    all_terms = terms * n_col
    pieces = width // LANES
    height = rows // HALVES
    last = pieces * HALVES - 1
    chunks = [(p, r) for p in range(pieces) for r in range(HALVES)]
    even = lax.rem(b, 2) == 0
    pair = b + 1 - 2 * lax.rem(b, 2)
    onward = b + 2 - 4 * lax.rem(b, 2)
    source = b - 2 + 4 * lax.rem(b, 2)
    has_onward = (onward >= 0) & (onward < n_blk)
    opposite = b - 1 + 2 * lax.rem(b, 2)
    has_source = (source >= 0) & (source < n_blk)
    my_rows = pl.ds(pl.multiple_of(c * rows, 16), rows)

    load_psi = pltpu.make_async_copy(psi, raw, local_sem.at[0])
    load_psi.start()
    load_dims = pltpu.make_async_copy(dims_in, dims, local_sem.at[3])
    load_dims.start()
    load_pattern = pltpu.make_async_copy(pattern_in, pattern, local_sem.at[4])
    load_pattern.start()
    load_left = pltpu.make_async_copy(
        left_env.at[:, :, my_rows, :], left.at[:, pl.ds(c * terms, terms)], local_sem.at[1]
    )
    load_left.start()
    load_right = pltpu.make_async_copy(
        right_env, right.at[pl.ds(c * terms, terms)], local_sem.at[2]
    )
    load_right.start()

    barrier = pltpu.get_barrier_semaphore()

    side = lax.rem(b, 2)
    mates, others = 2 * n_col, n_blk // 2

    def mate(m):
        f = lax.rem(side * n_col + c + m, mates)
        return (b - side + f // n_col, lax.rem(f, n_col))

    def other(m):
        return (lax.rem(b + 2 * m, n_blk), c)

    @pl.when(has_source)
    def _():
        pl.semaphore_signal(barrier, inc=1, device_id=(opposite, c), device_id_type=MESH)

    @pl.loop(1, others)
    def _(m):
        pl.semaphore_signal(barrier, inc=1, device_id=other(m), device_id_type=MESH)

    for m in range(1, mates):
        pl.semaphore_signal(barrier, inc=1, device_id=mate(m), device_id_type=MESH)

    load_dims.wait()
    load_pattern.wait()
    load_psi.wait()
    row_ids = c * rows + lax.broadcasted_iota(jnp.int32, (rows, width), 0)
    col_ids = lax.broadcasted_iota(jnp.int32, (rows, width), 1)
    furthest = jnp.maximum(row_ids, col_ids)
    for s in range(sectors):
        masked_psi = jnp.where(furthest < dims[s], raw[s].astype(jnp.float32), 0.0)
        for i, (p, r) in enumerate(chunks):
            own[0, i, s] = masked_psi[
                r * height : (r + 1) * height, p * LANES : (p + 1) * LANES
            ].astype(jnp.bfloat16)

    @pl.when(jnp.logical_not(has_source))
    def _():
        far[...] = jnp.zeros_like(far)

    pl.semaphore_wait(barrier, mates + others - 2 + has_source.astype(jnp.int32))

    def to_pair(h, i):
        return pltpu.make_async_remote_copy(
            src_ref=own.at[h, i],
            dst_ref=near.at[h, i],
            send_sem=near_send,
            recv_sem=near_recv.at[h, i],
            device_id=(pair, c),
            device_id_type=MESH,
        )

    def to_onward(h, i):
        count = rows // 2 if i == last else rows
        part = pl.ds(0, count)
        return pltpu.make_async_remote_copy(
            src_ref=near.at[h, i, :, part],
            dst_ref=far.at[h, i, :, part],
            send_sem=far_send.at[h, i],
            recv_sem=far_recv.at[h, i],
            device_id=(onward, c),
            device_id_type=MESH,
        )

    def direct(h):
        part = pl.ds(rows // 2, rows - rows // 2)
        return pltpu.make_async_remote_copy(
            src_ref=own.at[h, last, :, part],
            dst_ref=far.at[h, last, :, part],
            send_sem=direct_send.at[h],
            recv_sem=direct_recv.at[h],
            device_id=(opposite, c),
            device_id_type=MESH,
        )

    def start_halo(h):
        for i in range(len(chunks)):
            to_pair(h, i).start()

        @pl.when(has_source)
        def _():
            direct(h).start()

    def z_part(h, i, holder):
        p, r = chunks[i]
        start = pl.multiple_of(holder * rows + r * height, 16)
        return z.at[h, p, :, pl.ds(start, height), :]

    def z_copy(h, i, k, holder):
        return pltpu.make_async_remote_copy(
            src_ref=z_part(h, i, holder),
            dst_ref=z_part(h, i, holder),
            send_sem=z_send.at[k - 1],
            recv_sem=z_recv.at[h, k - 1, i],
            device_id=(b, lax.rem(c + k, n_col)),
            device_id_type=MESH,
        )

    def env_copies(k, holder, taker):
        took = pl.ds(pl.multiple_of(taker * rows, 16), rows)
        slot = pl.ds(holder * terms, terms)
        return [
            pltpu.make_async_remote_copy(
                src_ref=src,
                dst_ref=dst,
                send_sem=env_send.at[k - 1, j],
                recv_sem=env_recv.at[k - 1, j],
                device_id=(b, lax.rem(c + k, n_col)),
                device_id_type=MESH,
            )
            for j, (src, dst) in enumerate(
                [
                    (left_env.at[:, :, took, :], left.at[:, slot]),
                    (right_env, right.at[slot]),
                ]
            )
        ]

    start_halo(0)
    for k in range(1, n_col):
        for copy in env_copies(k, c, lax.rem(c + k, n_col)):
            copy.start()

    coeff = [[pattern[s, j].astype(jnp.float32) for j in range(5)] for s in range(2)]
    zero = jnp.float32(0.0)
    below = ((coeff[0][0], coeff[0][1]), (zero, coeff[1][0]))
    above = ((coeff[0][4], zero), (coeff[1][3], coeff[1][4]))
    inner = ((coeff[0][2], coeff[0][3]), (coeff[1][1], coeff[1][2]))
    near_c = [[jnp.where(even, above[s][k], below[s][k]) for k in range(2)] for s in range(2)]
    far_c = [[jnp.where(even, below[s][k], above[s][k]) for k in range(2)] for s in range(2)]

    def combine(h, i, theta):
        p, r = chunks[i]
        start = pl.multiple_of(c * rows + r * height, 16)
        total = [None, None]
        for ref, weights in ((own, inner), (near, near_c), (far, far_c)):
            for k in range(2):
                block = ref[h, i, k].astype(jnp.float32)
                for s in range(2):
                    term = weights[s][k] * block
                    total[s] = term if total[s] is None else total[s] + term
        for s in range(2):
            if h == 0:
                z_psi[i, s] = total[s]
            else:
                total[s] = total[s] - theta * z_psi[i, s]
            z[h, p, s, pl.ds(start, height), :] = total[s].astype(jnp.bfloat16)

    def product(h, p):
        temp = []
        for s in range(2):
            t = jnp.dot(
                left[s].reshape(all_terms * rows, width),
                z[h, p, s],
                preferred_element_type=jnp.float32,
            ).astype(jnp.bfloat16)
            temp.append(t)
        wide = jnp.concatenate(
            [
                jnp.concatenate([t[w * rows : (w + 1) * rows] for t in temp], axis=0)
                for w in range(all_terms)
            ],
            axis=1,
        )
        part = jnp.dot(wide, turned[p], preferred_element_type=jnp.float32)
        if p == 0:
            acc[...] = part
            return
        if p < pieces - 1:
            acc[...] += part
            return
        part = (part + acc[...]) * (1.0 / float(all_terms) ** 0.5)
        for s in range(2):
            block = jnp.where(furthest < dims[s], part[s * rows : (s + 1) * rows], 0.0)
            (first_out, second_out)[h][s] = block
            if h == 0:
                for i, (q, r) in enumerate(chunks):
                    own[1, i, s] = block[
                        r * height : (r + 1) * height, q * LANES : (q + 1) * LANES
                    ].astype(jnp.bfloat16)

    def finish_piece(h, p):
        for r in range(HALVES):
            for k in range(1, n_col):
                z_copy(h, p * HALVES + r, k, lax.rem(c + n_col - k, n_col)).wait_recv()
        product(h, p)

    def settle_env():
        load_left.wait()
        load_right.wait()
        for k in range(1, n_col):
            for copy in env_copies(k, lax.rem(c + n_col - k, n_col), c):
                copy.wait_recv()
        for p in range(pieces):
            for w in range(all_terms):
                turned[p, w * LANES : (w + 1) * LANES, :] = right[
                    w, :, p * LANES : (p + 1) * LANES
                ].T

    def apply(h, theta_of, lag):
        theta = None
        count = len(chunks)
        for i in range(count + lag + 1):
            if i < count:
                to_pair(h, i).wait_recv()

                @pl.when(has_onward)
                def _():
                    to_onward(h, i).start()

                if h == 0 and i == 0:
                    settle_env()

            j = i - lag
            if 0 <= j < count:

                @pl.when(has_source)
                def _():
                    to_onward(h, j).wait_recv()
                    if j == last:
                        direct(h).wait_recv()

                if j == 0 and theta_of is not None:
                    theta = theta_of()
                combine(h, j, theta)
                for k in range(1, n_col):
                    z_copy(h, j, k, c).start()
            j = i - lag - 1
            if j >= 0 and j % HALVES == HALVES - 1:
                finish_piece(h, j // HALVES)

    def settle(ref, sem):
        pltpu.make_async_copy(ref, ref, sem).wait()

    def inner_product(with_sigma):
        total = None
        for i, (p, r) in enumerate(chunks):
            for s in range(2):
                v = own[0, i, s].astype(jnp.float32)
                w = v
                if with_sigma:
                    w = first_out[
                        s, r * height : (r + 1) * height, p * LANES : (p + 1) * LANES
                    ]
                term = jnp.sum((v * w).reshape(height // 8, 8, LANES), axis=0)
                total = term if total is None else total + term
        return total

    stat_own[1] = inner_product(False)
    apply(0, None, 1)
    stat_own[0] = inner_product(True)

    def stat_to_mate(m):
        return pltpu.make_async_remote_copy(
            src_ref=stat_own,
            dst_ref=stat_mate.at[m - 1],
            send_sem=stat_sem.at[0],
            recv_sem=stat_sem.at[1],
            device_id=mate(m),
            device_id_type=MESH,
        )

    def stat_to_other(m):
        return pltpu.make_async_remote_copy(
            src_ref=stat_sum,
            dst_ref=stat_far.at[m - 1],
            send_sem=stat_sem.at[2],
            recv_sem=stat_sem.at[3],
            device_id=other(m),
            device_id_type=MESH,
        )

    for m in range(1, mates):
        stat_to_mate(m).start()
    start_halo(1)
    settle(stat_mate, stat_sem.at[1])
    stat_sum[...] = stat_own[...] + jnp.sum(stat_mate[...], axis=0)

    @pl.loop(1, others)
    def _(m):
        stat_to_other(m).start()

    def theta_of():
        settle(stat_far, stat_sem.at[3])
        total = stat_sum[...] + jnp.sum(stat_far[...], axis=0)
        sums = [jnp.sum(total[q], axis=(0, 1), keepdims=True) for q in range(2)]
        return sums[0] / sums[1]

    apply(1, theta_of, 1)

    settle(stat_mate, stat_sem.at[0])
    settle(stat_far, stat_sem.at[2])
    settle(own, near_send)

    @pl.when(has_onward)
    def _():
        for h in range(2):
            for i in range(len(chunks)):
                to_onward(h, i).wait_send()

    @pl.when(has_source)
    def _():
        for h in range(2):
            direct(h).wait_send()

    for k in range(1, n_col):
        settle(own, z_send.at[k - 1])
        for copy in env_copies(k, c, lax.rem(c + k, n_col)):
            copy.wait_send()


def body(n_blk, n_col, psi, dims, pattern, left_env, right_env):
    sectors, rows, width = psi.shape
    terms = left_env.shape[1] * n_col
    chunks = (width // LANES) * HALVES
    halo = (chunks, sectors, rows // HALVES, LANES)
    bf16, f32 = jnp.bfloat16, jnp.float32
    dma = pltpu.SemaphoreType.DMA
    vmem = pltpu.VMEM
    hbm = pl.BlockSpec(memory_space=pl.ANY)
    out = vmem(psi.shape, f32)
    return pl.pallas_call(
        functools.partial(kernel, n_blk, n_col),
        out_shape=(out, out),
        in_specs=[hbm] * 5,
        out_specs=(pl.BlockSpec(memory_space=vmem),) * 2,
        scratch_shapes=[
            pltpu.SMEM(dims.shape, jnp.int32),
            pltpu.SMEM(pattern.shape, jnp.int32),
            vmem((sectors, rows, width), bf16),
            vmem((2, *halo), bf16),
            vmem((2, *halo), bf16),
            vmem((2, *halo), bf16),
            vmem((2, width // LANES, sectors, width, LANES), bf16),
            vmem(halo, f32),
            vmem((sectors, terms, rows, width), bf16),
            vmem((terms, width, width), bf16),
            vmem((width // LANES, terms * LANES, width), bf16),
            vmem((sectors * rows, width), f32),
            vmem((2, 8, LANES), f32),
            vmem((2 * n_col - 1, 2, 8, LANES), f32),
            vmem((2, 8, LANES), f32),
            vmem((n_blk // 2 - 1, 2, 8, LANES), f32),
            dma((5,)),
            dma(()),
            dma((2, chunks)),
            dma((2, chunks)),
            dma((2, chunks)),
            dma((2,)),
            dma((2,)),
            dma((n_col - 1,)),
            dma((2, n_col - 1, chunks)),
            dma((n_col - 1, 2)),
            dma((n_col - 1, 2)),
            dma((4,)),
        ],
        compiler_params=pltpu.CompilerParams(
            collective_id=0, has_side_effects=True, vmem_limit_bytes=60 * 1024 * 1024
        ),
    )(dims, pattern, psi, left_env, right_env)


def solution(mesh):
    return jax.shard_map(
        functools.partial(body, mesh.shape["blk"], mesh.shape["col"]),
        mesh=mesh,
        in_specs=(
            P("blk", "col", None),
            P("blk"),
            P("blk", None),
            P("blk", "col", None, None),
            P("col", None, None),
        ),
        out_specs=(P("blk", "col", None), P("blk", "col", None)),
        check_vma=False,
    )
```

```python
import functools

import jax
import jax.numpy as jnp
from jax import lax
from jax.experimental import pallas as pl
from jax.experimental.pallas import tpu as pltpu
from jax.sharding import PartitionSpec as P

MESH = pl.DeviceIdType.MESH
LANES = 128
HALVES = 1


def kernel(
    n_blk,
    n_col,
    dims_in,
    pattern_in,
    psi,
    left_env,
    right_env,
    first_out,
    second_out,
    dims,
    pattern,
    raw,
    own,
    near,
    far,
    z,
    z_psi,
    early,
    left,
    right,
    turned,
    acc,
    stat_own,
    stat_mate,
    stat_sum,
    stat_far,
    local_sem,
    near_send,
    near_recv,
    far_send,
    far_recv,
    z_send,
    z_recv,
    env_send,
    env_recv,
    stat_sem,
):
    b = lax.axis_index("blk")
    c = lax.axis_index("col")
    sectors, rows, width = psi.shape
    terms = left_env.shape[1]
    all_terms = terms * n_col
    pieces = width // LANES
    height = rows // HALVES
    chunks = [(p, r) for p in range(pieces) for r in range(HALVES)]
    even = lax.rem(b, 2) == 0
    pair = b + 1 - 2 * lax.rem(b, 2)
    onward = b + 2 - 4 * lax.rem(b, 2)
    source = b - 2 + 4 * lax.rem(b, 2)
    has_onward = (onward >= 0) & (onward < n_blk)
    has_source = (source >= 0) & (source < n_blk)
    my_rows = pl.ds(pl.multiple_of(c * rows, 16), rows)

    load_psi = pltpu.make_async_copy(psi, raw, local_sem.at[0])
    load_psi.start()
    load_dims = pltpu.make_async_copy(dims_in, dims, local_sem.at[3])
    load_dims.start()
    load_pattern = pltpu.make_async_copy(pattern_in, pattern, local_sem.at[4])
    load_pattern.start()
    load_left = pltpu.make_async_copy(
        left_env.at[:, :, my_rows, :], left.at[:, pl.ds(c * terms, terms)], local_sem.at[1]
    )
    load_left.start()
    load_right = pltpu.make_async_copy(
        right_env, right.at[pl.ds(c * terms, terms)], local_sem.at[2]
    )
    load_right.start()

    barrier = pltpu.get_barrier_semaphore()

    side = lax.rem(b, 2)
    mates, others = 2 * n_col, n_blk // 2

    def mate(m):
        f = lax.rem(side * n_col + c + m, mates)
        return (b - side + f // n_col, lax.rem(f, n_col))

    def other(m):
        return (lax.rem(b + 2 * m, n_blk), c)

    @pl.loop(1, others)
    def _(m):
        pl.semaphore_signal(barrier, inc=1, device_id=other(m), device_id_type=MESH)

    for m in range(1, mates):
        pl.semaphore_signal(barrier, inc=1, device_id=mate(m), device_id_type=MESH)

    load_dims.wait()
    load_pattern.wait()
    load_psi.wait()
    row_ids = c * rows + lax.broadcasted_iota(jnp.int32, (rows, width), 0)
    col_ids = lax.broadcasted_iota(jnp.int32, (rows, width), 1)
    furthest = jnp.maximum(row_ids, col_ids)
    for s in range(sectors):
        masked_psi = jnp.where(furthest < dims[s], raw[s].astype(jnp.float32), 0.0)
        for i, (p, r) in enumerate(chunks):
            own[0, i, s] = masked_psi[
                r * height : (r + 1) * height, p * LANES : (p + 1) * LANES
            ].astype(jnp.bfloat16)

    @pl.when(jnp.logical_not(has_source))
    def _():
        far[...] = jnp.zeros_like(far)

    pl.semaphore_wait(barrier, mates + others - 2)

    def to_pair(h, i):
        return pltpu.make_async_remote_copy(
            src_ref=own.at[h, i],
            dst_ref=near.at[h, i],
            send_sem=near_send,
            recv_sem=near_recv.at[h, i],
            device_id=(pair, c),
            device_id_type=MESH,
        )

    def to_onward(h, i):
        return pltpu.make_async_remote_copy(
            src_ref=near.at[h, i],
            dst_ref=far.at[h, i],
            send_sem=far_send,
            recv_sem=far_recv.at[h, i],
            device_id=(onward, c),
            device_id_type=MESH,
        )

    def z_part(h, i, holder):
        p, r = chunks[i]
        start = pl.multiple_of(holder * rows + r * height, 16)
        return z.at[h, p, :, pl.ds(start, height), :]

    def z_copy(h, i, k, holder):
        return pltpu.make_async_remote_copy(
            src_ref=z_part(h, i, holder),
            dst_ref=z_part(h, i, holder),
            send_sem=z_send.at[k - 1],
            recv_sem=z_recv.at[h, k - 1, i],
            device_id=(b, lax.rem(c + k, n_col)),
            device_id_type=MESH,
        )

    def env_copies(k, holder, taker):
        took = pl.ds(pl.multiple_of(taker * rows, 16), rows)
        slot = pl.ds(holder * terms, terms)
        return [
            pltpu.make_async_remote_copy(
                src_ref=src,
                dst_ref=dst,
                send_sem=env_send.at[k - 1, j],
                recv_sem=env_recv.at[k - 1, j],
                device_id=(b, lax.rem(c + k, n_col)),
                device_id_type=MESH,
            )
            for j, (src, dst) in enumerate(
                [
                    (left_env.at[:, :, took, :], left.at[:, slot]),
                    (right_env, right.at[slot]),
                ]
            )
        ]

    for i in range(len(chunks)):
        to_pair(0, i).start()
    for k in range(1, n_col):
        for copy in env_copies(k, c, lax.rem(c + k, n_col)):
            copy.start()

    coeff = [[pattern[s, j].astype(jnp.float32) for j in range(5)] for s in range(2)]
    zero = jnp.float32(0.0)
    below = ((coeff[0][0], coeff[0][1]), (zero, coeff[1][0]))
    above = ((coeff[0][4], zero), (coeff[1][3], coeff[1][4]))
    inner = ((coeff[0][2], coeff[0][3]), (coeff[1][1], coeff[1][2]))
    near_c = [[jnp.where(even, above[s][k], below[s][k]) for k in range(2)] for s in range(2)]
    far_c = [[jnp.where(even, below[s][k], above[s][k]) for k in range(2)] for s in range(2)]

    def weigh(h, i, parts, total):
        for ref, weights in parts:
            for k in range(2):
                block = ref[h, i, k].astype(jnp.float32)
                for s in range(2):
                    term = weights[s][k] * block
                    total[s] = term if total[s] is None else total[s] + term
        return total

    def combine_near(h, i):
        total = weigh(h, i, ((own, inner), (near, near_c)), [None, None])
        for s in range(2):
            if h == 1:
                early[i, s] = total[s]
            else:
                z_psi[i, s] = total[s]

    def combine(h, i, theta):
        p, r = chunks[i]
        start = pl.multiple_of(c * rows + r * height, 16)
        ref = early if h == 1 else z_psi
        total = weigh(h, i, ((far, far_c),), [ref[i, s] for s in range(2)])
        for s in range(2):
            if h == 0:
                z_psi[i, s] = total[s]
            else:
                total[s] = total[s] - theta * z_psi[i, s]
            z[h, p, s, pl.ds(start, height), :] = total[s].astype(jnp.bfloat16)

    def product(h, p):
        temp = []
        for s in range(2):
            t = jnp.dot(
                left[s].reshape(all_terms * rows, width),
                z[h, p, s],
                preferred_element_type=jnp.float32,
            ).astype(jnp.bfloat16)
            temp.append(t)
        wide = jnp.concatenate(
            [
                jnp.concatenate([t[w * rows : (w + 1) * rows] for t in temp], axis=0)
                for w in range(all_terms)
            ],
            axis=1,
        )
        part = jnp.dot(wide, turned[p], preferred_element_type=jnp.float32)
        if p == 0:
            acc[...] = part
            return
        if p < pieces - 1:
            acc[...] += part
            return
        part = (part + acc[...]) * (1.0 / float(all_terms) ** 0.5)
        for s in range(2):
            block = jnp.where(furthest < dims[s], part[s * rows : (s + 1) * rows], 0.0)
            (first_out, second_out)[h][s] = block
            if h == 0:
                for i, (q, r) in enumerate(chunks):
                    own[1, i, s] = block[
                        r * height : (r + 1) * height, q * LANES : (q + 1) * LANES
                    ].astype(jnp.bfloat16)

    def finish_piece(h, p):
        for r in range(HALVES):
            for k in range(1, n_col):
                z_copy(h, p * HALVES + r, k, lax.rem(c + n_col - k, n_col)).wait_recv()
        product(h, p)

    def settle_env():
        load_left.wait()
        load_right.wait()
        for k in range(1, n_col):
            for copy in env_copies(k, lax.rem(c + n_col - k, n_col), c):
                copy.wait_recv()
        for p in range(pieces):
            for w in range(all_terms):
                turned[p, w * LANES : (w + 1) * LANES, :] = right[
                    w, :, p * LANES : (p + 1) * LANES
                ].T

    def apply(h, theta_of, lag):
        theta = None
        count = len(chunks)
        for i in range(count + lag + 1):
            if i < count:
                to_pair(h, i).wait_recv()

                @pl.when(has_onward)
                def _():
                    to_onward(h, i).start()

                combine_near(h, i)
                if h == 0 and i == 1:
                    settle_env()

            j = i - lag
            if 0 <= j < count:

                @pl.when(has_source)
                def _():
                    to_onward(h, j).wait_recv()

                if j == 0 and theta_of is not None:
                    theta = theta_of()
                combine(h, j, theta)
                for k in range(1, n_col):
                    z_copy(h, j, k, c).start()
            j = i - lag - 1
            if j >= 0 and j % HALVES == HALVES - 1:
                if h == 1 and j == count - 1:
                    settle_sends()
                finish_piece(h, j // HALVES)

    def settle(ref, sem):
        pltpu.make_async_copy(ref, ref, sem).wait()

    def inner_product(with_sigma):
        total = None
        for i, (p, r) in enumerate(chunks):
            for s in range(2):
                v = own[0, i, s].astype(jnp.float32)
                w = v
                if with_sigma:
                    w = first_out[
                        s, r * height : (r + 1) * height, p * LANES : (p + 1) * LANES
                    ]
                term = jnp.sum((v * w).reshape(height // 8, 8, LANES), axis=0)
                total = term if total is None else total + term
        return total

    stat_own[1] = inner_product(False)
    apply(0, None, 1)
    stat_own[0] = inner_product(True)

    def stat_to_mate(m):
        return pltpu.make_async_remote_copy(
            src_ref=stat_own,
            dst_ref=stat_mate.at[m - 1],
            send_sem=stat_sem.at[0],
            recv_sem=stat_sem.at[1],
            device_id=mate(m),
            device_id_type=MESH,
        )

    def stat_to_other(m):
        return pltpu.make_async_remote_copy(
            src_ref=stat_sum,
            dst_ref=stat_far.at[m - 1],
            send_sem=stat_sem.at[2],
            recv_sem=stat_sem.at[3],
            device_id=other(m),
            device_id_type=MESH,
        )

    for m in range(1, mates):
        stat_to_mate(m).start()
    for i in range(len(chunks)):
        to_pair(1, i).start()
    settle(stat_mate, stat_sem.at[1])
    stat_sum[...] = stat_own[...] + jnp.sum(stat_mate[...], axis=0)

    @pl.loop(1, others)
    def _(m):
        stat_to_other(m).start()

    def theta_of():
        settle(stat_far, stat_sem.at[3])
        total = stat_sum[...] + jnp.sum(stat_far[...], axis=0)
        sums = [jnp.sum(total[q], axis=(0, 1), keepdims=True) for q in range(2)]
        return sums[0] / sums[1]

    def settle_sends():
        settle(stat_mate, stat_sem.at[0])
        settle(stat_far, stat_sem.at[2])
        settle(own, near_send)

        @pl.when(has_onward)
        def _():
            settle(near, far_send)

        for k in range(1, n_col):
            for copy in env_copies(k, c, lax.rem(c + k, n_col)):
                copy.wait_send()

    apply(1, theta_of, 2)
    for k in range(1, n_col):
        settle(own, z_send.at[k - 1])


def body(n_blk, n_col, psi, dims, pattern, left_env, right_env):
    sectors, rows, width = psi.shape
    terms = left_env.shape[1] * n_col
    chunks = (width // LANES) * HALVES
    halo = (chunks, sectors, rows // HALVES, LANES)
    bf16, f32 = jnp.bfloat16, jnp.float32
    dma = pltpu.SemaphoreType.DMA
    vmem = pltpu.VMEM
    hbm = pl.BlockSpec(memory_space=pl.ANY)
    out = vmem(psi.shape, f32)
    return pl.pallas_call(
        functools.partial(kernel, n_blk, n_col),
        out_shape=(out, out),
        in_specs=[hbm] * 5,
        out_specs=(pl.BlockSpec(memory_space=vmem),) * 2,
        scratch_shapes=[
            pltpu.SMEM(dims.shape, jnp.int32),
            pltpu.SMEM(pattern.shape, jnp.int32),
            vmem((sectors, rows, width), bf16),
            vmem((2, *halo), bf16),
            vmem((2, *halo), bf16),
            vmem((2, *halo), bf16),
            vmem((2, width // LANES, sectors, width, LANES), bf16),
            vmem(halo, f32),
            vmem(halo, f32),
            vmem((sectors, terms, rows, width), bf16),
            vmem((terms, width, width), bf16),
            vmem((width // LANES, terms * LANES, width), bf16),
            vmem((sectors * rows, width), f32),
            vmem((2, 8, LANES), f32),
            vmem((2 * n_col - 1, 2, 8, LANES), f32),
            vmem((2, 8, LANES), f32),
            vmem((n_blk // 2 - 1, 2, 8, LANES), f32),
            dma((5,)),
            dma(()),
            dma((2, chunks)),
            dma(()),
            dma((2, chunks)),
            dma((n_col - 1,)),
            dma((2, n_col - 1, chunks)),
            dma((n_col - 1, 2)),
            dma((n_col - 1, 2)),
            dma((4,)),
        ],
        compiler_params=pltpu.CompilerParams(
            collective_id=0, has_side_effects=True, vmem_limit_bytes=60 * 1024 * 1024
        ),
    )(dims, pattern, psi, left_env, right_env)


def solution(mesh):
    return jax.shard_map(
        functools.partial(body, mesh.shape["blk"], mesh.shape["col"]),
        mesh=mesh,
        in_specs=(
            P("blk", "col", None),
            P("blk"),
            P("blk", None),
            P("blk", "col", None, None),
            P("col", None, None),
        ),
        out_specs=(P("blk", "col", None), P("blk", "col", None)),
        check_vma=False,
    )
```

```python
import functools

import jax
import jax.numpy as jnp
from jax import lax
from jax.experimental import pallas as pl
from jax.experimental.pallas import tpu as pltpu
from jax.sharding import PartitionSpec as P

MESH = pl.DeviceIdType.MESH
LANES = 128
HALVES = 2


def kernel(
    n_blk,
    n_col,
    dims_in,
    pattern_in,
    psi,
    left_env,
    right_env,
    first_out,
    second_out,
    dims,
    pattern,
    raw,
    own,
    near,
    far,
    z,
    z_psi,
    early,
    left,
    right,
    turned,
    acc,
    stat_own,
    stat_mate,
    stat_sum,
    stat_far,
    local_sem,
    near_send,
    near_recv,
    far_send,
    far_recv,
    z_send,
    z_recv,
    env_send,
    env_recv,
    stat_sem,
):
    b = lax.axis_index("blk")
    c = lax.axis_index("col")
    sectors, rows, width = psi.shape
    terms = left_env.shape[1]
    all_terms = terms * n_col
    pieces = width // LANES
    height = rows // HALVES
    chunks = [(p, r) for p in range(pieces) for r in range(HALVES)]
    even = lax.rem(b, 2) == 0
    pair = b + 1 - 2 * lax.rem(b, 2)
    onward = b + 2 - 4 * lax.rem(b, 2)
    source = b - 2 + 4 * lax.rem(b, 2)
    has_onward = (onward >= 0) & (onward < n_blk)
    has_source = (source >= 0) & (source < n_blk)
    my_rows = pl.ds(pl.multiple_of(c * rows, 16), rows)

    load_psi = pltpu.make_async_copy(psi, raw, local_sem.at[0])
    load_psi.start()
    load_dims = pltpu.make_async_copy(dims_in, dims, local_sem.at[3])
    load_dims.start()
    load_pattern = pltpu.make_async_copy(pattern_in, pattern, local_sem.at[4])
    load_pattern.start()
    load_left = pltpu.make_async_copy(
        left_env.at[:, :, my_rows, :], left.at[:, pl.ds(c * terms, terms)], local_sem.at[1]
    )
    load_left.start()
    load_right = pltpu.make_async_copy(
        right_env, right.at[pl.ds(c * terms, terms)], local_sem.at[2]
    )
    load_right.start()

    barrier = pltpu.get_barrier_semaphore()

    side = lax.rem(b, 2)
    mates, others = 2 * n_col, n_blk // 2

    def mate(m):
        f = lax.rem(side * n_col + c + m, mates)
        return (b - side + f // n_col, lax.rem(f, n_col))

    def other(m):
        return (lax.rem(b + 2 * m, n_blk), c)

    @pl.loop(1, others)
    def _(m):
        pl.semaphore_signal(barrier, inc=1, device_id=other(m), device_id_type=MESH)

    for m in range(1, mates):
        pl.semaphore_signal(barrier, inc=1, device_id=mate(m), device_id_type=MESH)

    load_dims.wait()
    load_pattern.wait()
    load_psi.wait()
    row_ids = c * rows + lax.broadcasted_iota(jnp.int32, (rows, width), 0)
    col_ids = lax.broadcasted_iota(jnp.int32, (rows, width), 1)
    furthest = jnp.maximum(row_ids, col_ids)
    for s in range(sectors):
        masked_psi = jnp.where(furthest < dims[s], raw[s].astype(jnp.float32), 0.0)
        for i, (p, r) in enumerate(chunks):
            own[0, i, s] = masked_psi[
                r * height : (r + 1) * height, p * LANES : (p + 1) * LANES
            ].astype(jnp.bfloat16)

    @pl.when(jnp.logical_not(has_source))
    def _():
        far[...] = jnp.zeros_like(far)

    pl.semaphore_wait(barrier, mates + others - 2)

    def to_pair(h, i):
        return pltpu.make_async_remote_copy(
            src_ref=own.at[h, i],
            dst_ref=near.at[h, i],
            send_sem=near_send,
            recv_sem=near_recv.at[h, i],
            device_id=(pair, c),
            device_id_type=MESH,
        )

    def to_onward(h, i):
        return pltpu.make_async_remote_copy(
            src_ref=near.at[h, i],
            dst_ref=far.at[h, i],
            send_sem=far_send,
            recv_sem=far_recv.at[h, i],
            device_id=(onward, c),
            device_id_type=MESH,
        )

    def z_part(h, i, holder):
        p, r = chunks[i]
        start = pl.multiple_of(holder * rows + r * height, 16)
        return z.at[h, p, :, pl.ds(start, height), :]

    def z_copy(h, i, k, holder):
        return pltpu.make_async_remote_copy(
            src_ref=z_part(h, i, holder),
            dst_ref=z_part(h, i, holder),
            send_sem=z_send.at[k - 1],
            recv_sem=z_recv.at[h, k - 1, i],
            device_id=(b, lax.rem(c + k, n_col)),
            device_id_type=MESH,
        )

    def env_copies(k, holder, taker):
        took = pl.ds(pl.multiple_of(taker * rows, 16), rows)
        slot = pl.ds(holder * terms, terms)
        return [
            pltpu.make_async_remote_copy(
                src_ref=src,
                dst_ref=dst,
                send_sem=env_send.at[k - 1, j],
                recv_sem=env_recv.at[k - 1, j],
                device_id=(b, lax.rem(c + k, n_col)),
                device_id_type=MESH,
            )
            for j, (src, dst) in enumerate(
                [
                    (left_env.at[:, :, took, :], left.at[:, slot]),
                    (right_env, right.at[slot]),
                ]
            )
        ]

    for i in range(len(chunks)):
        to_pair(0, i).start()
    for k in range(1, n_col):
        for copy in env_copies(k, c, lax.rem(c + k, n_col)):
            copy.start()

    coeff = [[pattern[s, j].astype(jnp.float32) for j in range(5)] for s in range(2)]
    zero = jnp.float32(0.0)
    below = ((coeff[0][0], coeff[0][1]), (zero, coeff[1][0]))
    above = ((coeff[0][4], zero), (coeff[1][3], coeff[1][4]))
    inner = ((coeff[0][2], coeff[0][3]), (coeff[1][1], coeff[1][2]))
    near_c = [[jnp.where(even, above[s][k], below[s][k]) for k in range(2)] for s in range(2)]
    far_c = [[jnp.where(even, below[s][k], above[s][k]) for k in range(2)] for s in range(2)]

    def weigh(h, i, parts, total):
        for ref, weights in parts:
            for k in range(2):
                block = ref[h, i, k].astype(jnp.float32)
                for s in range(2):
                    term = weights[s][k] * block
                    total[s] = term if total[s] is None else total[s] + term
        return total

    def combine_near(h, i):
        total = weigh(h, i, ((own, inner), (near, near_c)), [None, None])
        for s in range(2):
            if h == 1:
                early[i, s] = total[s]
            else:
                z_psi[i, s] = total[s]

    def combine(h, i, theta):
        p, r = chunks[i]
        start = pl.multiple_of(c * rows + r * height, 16)
        ref = early if h == 1 else z_psi
        total = weigh(h, i, ((far, far_c),), [ref[i, s] for s in range(2)])
        for s in range(2):
            if h == 0:
                z_psi[i, s] = total[s]
            else:
                total[s] = total[s] - theta * z_psi[i, s]
            z[h, p, s, pl.ds(start, height), :] = total[s].astype(jnp.bfloat16)

    def product(h, p):
        temp = []
        for s in range(2):
            t = jnp.dot(
                left[s].reshape(all_terms * rows, width),
                z[h, p, s],
                preferred_element_type=jnp.float32,
            ).astype(jnp.bfloat16)
            temp.append(t)
        wide = jnp.concatenate(
            [
                jnp.concatenate([t[w * rows : (w + 1) * rows] for t in temp], axis=0)
                for w in range(all_terms)
            ],
            axis=1,
        )
        part = jnp.dot(wide, turned[p], preferred_element_type=jnp.float32)
        if p == 0:
            acc[...] = part
            return
        if p < pieces - 1:
            acc[...] += part
            return
        part = (part + acc[...]) * (1.0 / float(all_terms) ** 0.5)
        for s in range(2):
            block = jnp.where(furthest < dims[s], part[s * rows : (s + 1) * rows], 0.0)
            (first_out, second_out)[h][s] = block
            if h == 0:
                for i, (q, r) in enumerate(chunks):
                    own[1, i, s] = block[
                        r * height : (r + 1) * height, q * LANES : (q + 1) * LANES
                    ].astype(jnp.bfloat16)

    def finish_piece(h, p):
        for r in range(HALVES):
            for k in range(1, n_col):
                z_copy(h, p * HALVES + r, k, lax.rem(c + n_col - k, n_col)).wait_recv()
        product(h, p)

    def settle_env():
        load_left.wait()
        load_right.wait()
        for k in range(1, n_col):
            for copy in env_copies(k, lax.rem(c + n_col - k, n_col), c):
                copy.wait_recv()
        for p in range(pieces):
            for w in range(all_terms):
                turned[p, w * LANES : (w + 1) * LANES, :] = right[
                    w, :, p * LANES : (p + 1) * LANES
                ].T

    def apply(h, theta_of, lag):
        theta = None
        count = len(chunks)
        for i in range(count + lag + 1):
            if i < count:
                to_pair(h, i).wait_recv()

                @pl.when(has_onward)
                def _():
                    to_onward(h, i).start()

                combine_near(h, i)
                if h == 0 and i == 2 * HALVES - 1:
                    settle_env()

            j = i - lag
            if 0 <= j < count:

                @pl.when(has_source)
                def _():
                    to_onward(h, j).wait_recv()

                if j == 0 and theta_of is not None:
                    theta = theta_of()
                combine(h, j, theta)
                for k in range(1, n_col):
                    z_copy(h, j, k, c).start()
            j = i - lag - 1
            if j >= 0 and j % HALVES == HALVES - 1:
                if h == 1 and j == count - 1:
                    settle_sends()
                finish_piece(h, j // HALVES)

    def settle(ref, sem):
        pltpu.make_async_copy(ref, ref, sem).wait()

    def inner_product(with_sigma):
        total = None
        for i, (p, r) in enumerate(chunks):
            for s in range(2):
                v = own[0, i, s].astype(jnp.float32)
                w = v
                if with_sigma:
                    w = first_out[
                        s, r * height : (r + 1) * height, p * LANES : (p + 1) * LANES
                    ]
                term = jnp.sum((v * w).reshape(height // 8, 8, LANES), axis=0)
                total = term if total is None else total + term
        return total

    stat_own[1] = inner_product(False)
    apply(0, None, 1)
    stat_own[0] = inner_product(True)

    def stat_to_mate(m):
        return pltpu.make_async_remote_copy(
            src_ref=stat_own,
            dst_ref=stat_mate.at[m - 1],
            send_sem=stat_sem.at[0],
            recv_sem=stat_sem.at[1],
            device_id=mate(m),
            device_id_type=MESH,
        )

    def stat_to_other(m):
        return pltpu.make_async_remote_copy(
            src_ref=stat_sum,
            dst_ref=stat_far.at[m - 1],
            send_sem=stat_sem.at[2],
            recv_sem=stat_sem.at[3],
            device_id=other(m),
            device_id_type=MESH,
        )

    for m in range(1, mates):
        stat_to_mate(m).start()
    for i in range(len(chunks)):
        to_pair(1, i).start()
    settle(stat_mate, stat_sem.at[1])
    stat_sum[...] = stat_own[...] + jnp.sum(stat_mate[...], axis=0)

    @pl.loop(1, others)
    def _(m):
        stat_to_other(m).start()

    def theta_of():
        settle(stat_far, stat_sem.at[3])
        total = stat_sum[...] + jnp.sum(stat_far[...], axis=0)
        sums = [jnp.sum(total[q], axis=(0, 1), keepdims=True) for q in range(2)]
        return sums[0] / sums[1]

    def settle_sends():
        settle(stat_mate, stat_sem.at[0])
        settle(stat_far, stat_sem.at[2])
        settle(own, near_send)

        @pl.when(has_onward)
        def _():
            settle(near, far_send)

        for k in range(1, n_col):
            for copy in env_copies(k, c, lax.rem(c + k, n_col)):
                copy.wait_send()

    apply(1, theta_of, 3)
    for k in range(1, n_col):
        settle(own, z_send.at[k - 1])


def body(n_blk, n_col, psi, dims, pattern, left_env, right_env):
    sectors, rows, width = psi.shape
    terms = left_env.shape[1] * n_col
    chunks = (width // LANES) * HALVES
    halo = (chunks, sectors, rows // HALVES, LANES)
    bf16, f32 = jnp.bfloat16, jnp.float32
    dma = pltpu.SemaphoreType.DMA
    vmem = pltpu.VMEM
    hbm = pl.BlockSpec(memory_space=pl.ANY)
    out = vmem(psi.shape, f32)
    return pl.pallas_call(
        functools.partial(kernel, n_blk, n_col),
        out_shape=(out, out),
        in_specs=[hbm] * 5,
        out_specs=(pl.BlockSpec(memory_space=vmem),) * 2,
        scratch_shapes=[
            pltpu.SMEM(dims.shape, jnp.int32),
            pltpu.SMEM(pattern.shape, jnp.int32),
            vmem((sectors, rows, width), bf16),
            vmem((2, *halo), bf16),
            vmem((2, *halo), bf16),
            vmem((2, *halo), bf16),
            vmem((2, width // LANES, sectors, width, LANES), bf16),
            vmem(halo, f32),
            vmem(halo, f32),
            vmem((sectors, terms, rows, width), bf16),
            vmem((terms, width, width), bf16),
            vmem((width // LANES, terms * LANES, width), bf16),
            vmem((sectors * rows, width), f32),
            vmem((2, 8, LANES), f32),
            vmem((2 * n_col - 1, 2, 8, LANES), f32),
            vmem((2, 8, LANES), f32),
            vmem((n_blk // 2 - 1, 2, 8, LANES), f32),
            dma((5,)),
            dma(()),
            dma((2, chunks)),
            dma(()),
            dma((2, chunks)),
            dma((n_col - 1,)),
            dma((2, n_col - 1, chunks)),
            dma((n_col - 1, 2)),
            dma((n_col - 1, 2)),
            dma((4,)),
        ],
        compiler_params=pltpu.CompilerParams(
            collective_id=0, has_side_effects=True, vmem_limit_bytes=60 * 1024 * 1024
        ),
    )(dims, pattern, psi, left_env, right_env)


def solution(mesh):
    return jax.shard_map(
        functools.partial(body, mesh.shape["blk"], mesh.shape["col"]),
        mesh=mesh,
        in_specs=(
            P("blk", "col", None),
            P("blk"),
            P("blk", None),
            P("blk", "col", None, None),
            P("col", None, None),
        ),
        out_specs=(P("blk", "col", None), P("blk", "col", None)),
        check_vma=False,
    )
```

```python
import functools

import jax
import jax.numpy as jnp
from jax import lax
from jax.experimental import pallas as pl
from jax.experimental.pallas import tpu as pltpu
from jax.sharding import PartitionSpec as P

MESH = pl.DeviceIdType.MESH
LANES = 128
HALVES = 1


def kernel(
    n_blk,
    n_col,
    dims_in,
    pattern_in,
    psi,
    left_env,
    right_env,
    first_out,
    second_out,
    dims,
    pattern,
    raw,
    own,
    near,
    far,
    z,
    z_psi,
    early,
    left,
    right,
    turned,
    acc,
    stat_own,
    stat_mate,
    stat_sum,
    stat_far,
    local_sem,
    near_send,
    near_recv,
    far_send,
    far_recv,
    z_send,
    z_recv,
    env_send,
    env_recv,
    stat_sem,
):
    b = lax.axis_index("blk")
    c = lax.axis_index("col")
    sectors, rows, width = psi.shape
    terms = left_env.shape[1]
    all_terms = terms * n_col
    pieces = width // LANES
    height = rows // HALVES
    chunks = [(p, r) for p in range(pieces) for r in range(HALVES)]
    even = lax.rem(b, 2) == 0
    pair = b + 1 - 2 * lax.rem(b, 2)
    onward = b + 2 - 4 * lax.rem(b, 2)
    source = b - 2 + 4 * lax.rem(b, 2)
    has_onward = (onward >= 0) & (onward < n_blk)
    has_source = (source >= 0) & (source < n_blk)
    my_rows = pl.ds(pl.multiple_of(c * rows, 16), rows)

    load_psi = pltpu.make_async_copy(psi, raw, local_sem.at[0])
    load_psi.start()
    load_dims = pltpu.make_async_copy(dims_in, dims, local_sem.at[3])
    load_dims.start()
    load_pattern = pltpu.make_async_copy(pattern_in, pattern, local_sem.at[4])
    load_pattern.start()
    load_left = pltpu.make_async_copy(
        left_env.at[:, :, my_rows, :], left.at[:, pl.ds(c * terms, terms)], local_sem.at[1]
    )
    load_left.start()
    load_right = pltpu.make_async_copy(
        right_env, right.at[pl.ds(c * terms, terms)], local_sem.at[2]
    )
    load_right.start()

    barrier = pltpu.get_barrier_semaphore()

    side = lax.rem(b, 2)
    mates, others = 2 * n_col, n_blk // 2

    def mate(m):
        f = lax.rem(side * n_col + c + m, mates)
        return (b - side + f // n_col, lax.rem(f, n_col))

    def other(m):
        return (lax.rem(b + 2 * m, n_blk), c)

    @pl.loop(1, others)
    def _(m):
        pl.semaphore_signal(barrier, inc=1, device_id=other(m), device_id_type=MESH)

    for m in range(1, mates):
        pl.semaphore_signal(barrier, inc=1, device_id=mate(m), device_id_type=MESH)

    load_dims.wait()
    load_pattern.wait()
    load_psi.wait()
    row_ids = c * rows + lax.broadcasted_iota(jnp.int32, (rows, width), 0)
    col_ids = lax.broadcasted_iota(jnp.int32, (rows, width), 1)
    furthest = jnp.maximum(row_ids, col_ids)
    for s in range(sectors):
        masked_psi = jnp.where(furthest < dims[s], raw[s].astype(jnp.float32), 0.0)
        for i, (p, r) in enumerate(chunks):
            own[0, i, s] = masked_psi[
                r * height : (r + 1) * height, p * LANES : (p + 1) * LANES
            ].astype(jnp.bfloat16)

    @pl.when(jnp.logical_not(has_source))
    def _():
        far[...] = jnp.zeros_like(far)

    pl.semaphore_wait(barrier, mates + others - 2)

    def to_pair(h, i):
        return pltpu.make_async_remote_copy(
            src_ref=own.at[h, i],
            dst_ref=near.at[h, i],
            send_sem=near_send,
            recv_sem=near_recv.at[h, i],
            device_id=(pair, c),
            device_id_type=MESH,
        )

    def to_onward(h, i):
        return pltpu.make_async_remote_copy(
            src_ref=near.at[h, i],
            dst_ref=far.at[h, i],
            send_sem=far_send,
            recv_sem=far_recv.at[h, i],
            device_id=(onward, c),
            device_id_type=MESH,
        )

    first_core = lax.rem(c, 2) == 0

    def start_halo(h):
        to_pair(h, 0).start()

        @pl.when(first_core)
        def _():
            for i in range(1, len(chunks)):
                to_pair(h, i).start()

    def z_part(h, i, holder):
        p, r = chunks[i]
        start = pl.multiple_of(holder * rows + r * height, 16)
        return z.at[h, p, :, pl.ds(start, height), :]

    def z_copy(h, i, k, holder):
        return pltpu.make_async_remote_copy(
            src_ref=z_part(h, i, holder),
            dst_ref=z_part(h, i, holder),
            send_sem=z_send.at[k - 1],
            recv_sem=z_recv.at[h, k - 1, i],
            device_id=(b, lax.rem(c + k, n_col)),
            device_id_type=MESH,
        )

    def env_copies(k, holder, taker):
        took = pl.ds(pl.multiple_of(taker * rows, 16), rows)
        slot = pl.ds(holder * terms, terms)
        return [
            pltpu.make_async_remote_copy(
                src_ref=src,
                dst_ref=dst,
                send_sem=env_send.at[k - 1, j],
                recv_sem=env_recv.at[k - 1, j],
                device_id=(b, lax.rem(c + k, n_col)),
                device_id_type=MESH,
            )
            for j, (src, dst) in enumerate(
                [
                    (left_env.at[:, :, took, :], left.at[:, slot]),
                    (right_env, right.at[slot]),
                ]
            )
        ]

    start_halo(0)
    for k in range(1, n_col):
        for copy in env_copies(k, c, lax.rem(c + k, n_col)):
            copy.start()

    coeff = [[pattern[s, j].astype(jnp.float32) for j in range(5)] for s in range(2)]
    zero = jnp.float32(0.0)
    below = ((coeff[0][0], coeff[0][1]), (zero, coeff[1][0]))
    above = ((coeff[0][4], zero), (coeff[1][3], coeff[1][4]))
    inner = ((coeff[0][2], coeff[0][3]), (coeff[1][1], coeff[1][2]))
    near_c = [[jnp.where(even, above[s][k], below[s][k]) for k in range(2)] for s in range(2)]
    far_c = [[jnp.where(even, below[s][k], above[s][k]) for k in range(2)] for s in range(2)]

    def weigh(h, i, parts, total):
        for ref, weights in parts:
            for k in range(2):
                block = ref[h, i, k].astype(jnp.float32)
                for s in range(2):
                    term = weights[s][k] * block
                    total[s] = term if total[s] is None else total[s] + term
        return total

    def combine_near(h, i):
        total = weigh(h, i, ((own, inner), (near, near_c)), [None, None])
        for s in range(2):
            if h == 1:
                early[i, s] = total[s]
            else:
                z_psi[i, s] = total[s]

    def combine(h, i, theta):
        p, r = chunks[i]
        start = pl.multiple_of(c * rows + r * height, 16)
        ref = early if h == 1 else z_psi
        total = weigh(h, i, ((far, far_c),), [ref[i, s] for s in range(2)])
        for s in range(2):
            if h == 0:
                z_psi[i, s] = total[s]
            else:
                total[s] = total[s] - theta * z_psi[i, s]
            z[h, p, s, pl.ds(start, height), :] = total[s].astype(jnp.bfloat16)

    def product(h, p):
        temp = []
        for s in range(2):
            t = jnp.dot(
                left[s].reshape(all_terms * rows, width),
                z[h, p, s],
                preferred_element_type=jnp.float32,
            ).astype(jnp.bfloat16)
            temp.append(t)
        wide = jnp.concatenate(
            [
                jnp.concatenate([t[w * rows : (w + 1) * rows] for t in temp], axis=0)
                for w in range(all_terms)
            ],
            axis=1,
        )
        part = jnp.dot(wide, turned[p], preferred_element_type=jnp.float32)
        if p == 0:
            acc[...] = part
            return
        if p < pieces - 1:
            acc[...] += part
            return
        part = (part + acc[...]) * (1.0 / float(all_terms) ** 0.5)
        for s in range(2):
            block = jnp.where(furthest < dims[s], part[s * rows : (s + 1) * rows], 0.0)
            (first_out, second_out)[h][s] = block
            if h == 0:
                for i, (q, r) in enumerate(chunks):
                    own[1, i, s] = block[
                        r * height : (r + 1) * height, q * LANES : (q + 1) * LANES
                    ].astype(jnp.bfloat16)

    def finish_piece(h, p):
        for r in range(HALVES):
            for k in range(1, n_col):
                z_copy(h, p * HALVES + r, k, lax.rem(c + n_col - k, n_col)).wait_recv()
        product(h, p)

    def settle_env():
        load_left.wait()
        load_right.wait()
        for k in range(1, n_col):
            for copy in env_copies(k, lax.rem(c + n_col - k, n_col), c):
                copy.wait_recv()
        for p in range(pieces):
            for w in range(all_terms):
                turned[p, w * LANES : (w + 1) * LANES, :] = right[
                    w, :, p * LANES : (p + 1) * LANES
                ].T

    def apply(h, theta_of, lag):
        theta = None
        count = len(chunks)
        for i in range(count + lag + 1):
            if i < count:
                to_pair(h, i).wait_recv()

                @pl.when(has_onward)
                def _():
                    to_onward(h, i).start()

                if i == 0:

                    @pl.when(jnp.logical_not(first_core))
                    def _():
                        for m in range(1, count):
                            to_pair(h, m).start()

                combine_near(h, i)
                if h == 0 and i == 1:
                    settle_env()

            j = i - lag
            if 0 <= j < count:

                @pl.when(has_source)
                def _():
                    to_onward(h, j).wait_recv()

                if j == 0 and theta_of is not None:
                    theta = theta_of()
                combine(h, j, theta)
                for k in range(1, n_col):
                    z_copy(h, j, k, c).start()
            j = i - lag - 1
            if j >= 0 and j % HALVES == HALVES - 1:
                if h == 1 and j == count - 1:
                    settle_sends()
                finish_piece(h, j // HALVES)

    def settle(ref, sem):
        pltpu.make_async_copy(ref, ref, sem).wait()

    def inner_product(with_sigma):
        total = None
        for i, (p, r) in enumerate(chunks):
            for s in range(2):
                v = own[0, i, s].astype(jnp.float32)
                w = v
                if with_sigma:
                    w = first_out[
                        s, r * height : (r + 1) * height, p * LANES : (p + 1) * LANES
                    ]
                term = jnp.sum((v * w).reshape(height // 8, 8, LANES), axis=0)
                total = term if total is None else total + term
        return total

    stat_own[1] = inner_product(False)
    apply(0, None, 1)
    stat_own[0] = inner_product(True)

    def stat_to_mate(m):
        return pltpu.make_async_remote_copy(
            src_ref=stat_own,
            dst_ref=stat_mate.at[m - 1],
            send_sem=stat_sem.at[0],
            recv_sem=stat_sem.at[1],
            device_id=mate(m),
            device_id_type=MESH,
        )

    def stat_to_other(m):
        return pltpu.make_async_remote_copy(
            src_ref=stat_sum,
            dst_ref=stat_far.at[m - 1],
            send_sem=stat_sem.at[2],
            recv_sem=stat_sem.at[3],
            device_id=other(m),
            device_id_type=MESH,
        )

    for m in range(1, mates):
        stat_to_mate(m).start()
    start_halo(1)
    settle(stat_mate, stat_sem.at[1])
    stat_sum[...] = stat_own[...] + jnp.sum(stat_mate[...], axis=0)

    @pl.loop(1, others)
    def _(m):
        stat_to_other(m).start()

    def theta_of():
        settle(stat_far, stat_sem.at[3])
        total = stat_sum[...] + jnp.sum(stat_far[...], axis=0)
        sums = [jnp.sum(total[q], axis=(0, 1), keepdims=True) for q in range(2)]
        return sums[0] / sums[1]

    def settle_sends():
        settle(stat_mate, stat_sem.at[0])
        settle(stat_far, stat_sem.at[2])
        settle(own, near_send)

        @pl.when(has_onward)
        def _():
            settle(near, far_send)

        for k in range(1, n_col):
            for copy in env_copies(k, c, lax.rem(c + k, n_col)):
                copy.wait_send()

    apply(1, theta_of, 2)
    for k in range(1, n_col):
        settle(own, z_send.at[k - 1])


def body(n_blk, n_col, psi, dims, pattern, left_env, right_env):
    sectors, rows, width = psi.shape
    terms = left_env.shape[1] * n_col
    chunks = (width // LANES) * HALVES
    halo = (chunks, sectors, rows // HALVES, LANES)
    bf16, f32 = jnp.bfloat16, jnp.float32
    dma = pltpu.SemaphoreType.DMA
    vmem = pltpu.VMEM
    hbm = pl.BlockSpec(memory_space=pl.ANY)
    out = vmem(psi.shape, f32)
    return pl.pallas_call(
        functools.partial(kernel, n_blk, n_col),
        out_shape=(out, out),
        in_specs=[hbm] * 5,
        out_specs=(pl.BlockSpec(memory_space=vmem),) * 2,
        scratch_shapes=[
            pltpu.SMEM(dims.shape, jnp.int32),
            pltpu.SMEM(pattern.shape, jnp.int32),
            vmem((sectors, rows, width), bf16),
            vmem((2, *halo), bf16),
            vmem((2, *halo), bf16),
            vmem((2, *halo), bf16),
            vmem((2, width // LANES, sectors, width, LANES), bf16),
            vmem(halo, f32),
            vmem(halo, f32),
            vmem((sectors, terms, rows, width), bf16),
            vmem((terms, width, width), bf16),
            vmem((width // LANES, terms * LANES, width), bf16),
            vmem((sectors * rows, width), f32),
            vmem((2, 8, LANES), f32),
            vmem((2 * n_col - 1, 2, 8, LANES), f32),
            vmem((2, 8, LANES), f32),
            vmem((n_blk // 2 - 1, 2, 8, LANES), f32),
            dma((5,)),
            dma(()),
            dma((2, chunks)),
            dma(()),
            dma((2, chunks)),
            dma((n_col - 1,)),
            dma((2, n_col - 1, chunks)),
            dma((n_col - 1, 2)),
            dma((n_col - 1, 2)),
            dma((4,)),
        ],
        compiler_params=pltpu.CompilerParams(
            collective_id=0, has_side_effects=True, vmem_limit_bytes=60 * 1024 * 1024
        ),
    )(dims, pattern, psi, left_env, right_env)


def solution(mesh):
    return jax.shard_map(
        functools.partial(body, mesh.shape["blk"], mesh.shape["col"]),
        mesh=mesh,
        in_specs=(
            P("blk", "col", None),
            P("blk"),
            P("blk", None),
            P("blk", "col", None, None),
            P("col", None, None),
        ),
        out_specs=(P("blk", "col", None), P("blk", "col", None)),
        check_vma=False,
    )
```

```python
import functools

import jax
import jax.numpy as jnp
from jax import lax
from jax.experimental import pallas as pl
from jax.experimental.pallas import tpu as pltpu
from jax.sharding import PartitionSpec as P

MESH = pl.DeviceIdType.MESH
LANES = 128
HALVES = 1


def kernel(
    n_blk,
    n_col,
    dims_in,
    pattern_in,
    psi,
    left_env,
    right_env,
    first_out,
    second_out,
    dims,
    pattern,
    raw,
    own,
    near,
    far,
    z,
    z_psi,
    early,
    left,
    right,
    turned,
    acc,
    stat_own,
    stat_mate,
    stat_sum,
    stat_far,
    local_sem,
    near_send,
    near_recv,
    far_send,
    far_recv,
    z_send,
    z_recv,
    env_send,
    env_recv,
    stat_sem,
):
    b = lax.axis_index("blk")
    c = lax.axis_index("col")
    sectors, rows, width = psi.shape
    terms = left_env.shape[1]
    all_terms = terms * n_col
    pieces = width // LANES
    height = rows // HALVES
    chunks = [(p, r) for p in range(pieces) for r in range(HALVES)]
    even = lax.rem(b, 2) == 0
    pair = b + 1 - 2 * lax.rem(b, 2)
    onward = b + 2 - 4 * lax.rem(b, 2)
    source = b - 2 + 4 * lax.rem(b, 2)
    has_onward = (onward >= 0) & (onward < n_blk)
    has_source = (source >= 0) & (source < n_blk)
    my_rows = pl.ds(pl.multiple_of(c * rows, 16), rows)

    load_psi = pltpu.make_async_copy(psi, raw, local_sem.at[0])
    load_psi.start()
    load_dims = pltpu.make_async_copy(dims_in, dims, local_sem.at[3])
    load_dims.start()
    load_pattern = pltpu.make_async_copy(pattern_in, pattern, local_sem.at[4])
    load_pattern.start()
    load_left = pltpu.make_async_copy(
        left_env.at[:, :, my_rows, :], left.at[:, pl.ds(c * terms, terms)], local_sem.at[1]
    )
    load_left.start()
    load_right = pltpu.make_async_copy(
        right_env, right.at[pl.ds(c * terms, terms)], local_sem.at[2]
    )
    load_right.start()

    barrier = pltpu.get_barrier_semaphore()

    side = lax.rem(b, 2)
    mates, others = 2 * n_col, n_blk // 2

    def mate(m):
        f = lax.rem(side * n_col + c + m, mates)
        return (b - side + f // n_col, lax.rem(f, n_col))

    def other(m):
        return (lax.rem(b + 2 * m, n_blk), c)

    @pl.loop(1, others)
    def _(m):
        pl.semaphore_signal(barrier, inc=1, device_id=other(m), device_id_type=MESH)

    for m in range(1, mates):
        pl.semaphore_signal(barrier, inc=1, device_id=mate(m), device_id_type=MESH)

    load_dims.wait()
    load_pattern.wait()
    load_psi.wait()
    row_ids = c * rows + lax.broadcasted_iota(jnp.int32, (rows, width), 0)
    col_ids = lax.broadcasted_iota(jnp.int32, (rows, width), 1)
    furthest = jnp.maximum(row_ids, col_ids)
    for s in range(sectors):
        masked_psi = jnp.where(furthest < dims[s], raw[s].astype(jnp.float32), 0.0)
        for i, (p, r) in enumerate(chunks):
            own[0, i, s] = masked_psi[
                r * height : (r + 1) * height, p * LANES : (p + 1) * LANES
            ].astype(jnp.bfloat16)

    @pl.when(jnp.logical_not(has_source))
    def _():
        far[...] = jnp.zeros_like(far)

    pl.semaphore_wait(barrier, mates + others - 2)

    def to_pair(h, i):
        return pltpu.make_async_remote_copy(
            src_ref=own.at[h, i],
            dst_ref=near.at[h, i],
            send_sem=near_send,
            recv_sem=near_recv.at[h, i],
            device_id=(pair, c),
            device_id_type=MESH,
        )

    def to_onward(h, i):
        return pltpu.make_async_remote_copy(
            src_ref=near.at[h, i],
            dst_ref=far.at[h, i],
            send_sem=far_send,
            recv_sem=far_recv.at[h, i],
            device_id=(onward, c),
            device_id_type=MESH,
        )

    first_core = lax.rem(c, 2) == 0

    def start_halo(h):
        to_pair(h, 0).start()

        @pl.when(first_core)
        def _():
            for i in range(1, len(chunks)):
                to_pair(h, i).start()

    def z_part(h, i, holder):
        p, r = chunks[i]
        start = pl.multiple_of(holder * rows + r * height, 16)
        return z.at[h, p, :, pl.ds(start, height), :]

    def z_copy(h, i, k, holder):
        return pltpu.make_async_remote_copy(
            src_ref=z_part(h, i, holder),
            dst_ref=z_part(h, i, holder),
            send_sem=z_send.at[k - 1],
            recv_sem=z_recv.at[h, k - 1, i],
            device_id=(b, lax.rem(c + k, n_col)),
            device_id_type=MESH,
        )

    def env_copies(k, holder, taker):
        took = pl.ds(pl.multiple_of(taker * rows, 16), rows)
        slot = pl.ds(holder * terms, terms)
        return [
            pltpu.make_async_remote_copy(
                src_ref=src,
                dst_ref=dst,
                send_sem=env_send.at[k - 1, j],
                recv_sem=env_recv.at[k - 1, j],
                device_id=(b, lax.rem(c + k, n_col)),
                device_id_type=MESH,
            )
            for j, (src, dst) in enumerate(
                [
                    (left_env.at[:, :, took, :], left.at[:, slot]),
                    (right_env, right.at[slot]),
                ]
            )
        ]

    start_halo(0)

    def start_env():
        for k in range(1, n_col):
            for copy in env_copies(k, c, lax.rem(c + k, n_col)):
                copy.start()

    pl.when(jnp.logical_not(first_core))(start_env)

    coeff = [[pattern[s, j].astype(jnp.float32) for j in range(5)] for s in range(2)]
    zero = jnp.float32(0.0)
    below = ((coeff[0][0], coeff[0][1]), (zero, coeff[1][0]))
    above = ((coeff[0][4], zero), (coeff[1][3], coeff[1][4]))
    inner = ((coeff[0][2], coeff[0][3]), (coeff[1][1], coeff[1][2]))
    near_c = [[jnp.where(even, above[s][k], below[s][k]) for k in range(2)] for s in range(2)]
    far_c = [[jnp.where(even, below[s][k], above[s][k]) for k in range(2)] for s in range(2)]

    def weigh(h, i, parts, total):
        for ref, weights in parts:
            for k in range(2):
                block = ref[h, i, k].astype(jnp.float32)
                for s in range(2):
                    term = weights[s][k] * block
                    total[s] = term if total[s] is None else total[s] + term
        return total

    def combine_near(h, i):
        total = weigh(h, i, ((own, inner), (near, near_c)), [None, None])
        for s in range(2):
            if h == 1:
                early[i, s] = total[s]
            else:
                z_psi[i, s] = total[s]

    def combine(h, i, theta):
        p, r = chunks[i]
        start = pl.multiple_of(c * rows + r * height, 16)
        ref = early if h == 1 else z_psi
        total = weigh(h, i, ((far, far_c),), [ref[i, s] for s in range(2)])
        for s in range(2):
            if h == 0:
                z_psi[i, s] = total[s]
            else:
                total[s] = total[s] - theta * z_psi[i, s]
            z[h, p, s, pl.ds(start, height), :] = total[s].astype(jnp.bfloat16)

    def product(h, p):
        temp = []
        for s in range(2):
            t = jnp.dot(
                left[s].reshape(all_terms * rows, width),
                z[h, p, s],
                preferred_element_type=jnp.float32,
            ).astype(jnp.bfloat16)
            temp.append(t)
        wide = jnp.concatenate(
            [
                jnp.concatenate([t[w * rows : (w + 1) * rows] for t in temp], axis=0)
                for w in range(all_terms)
            ],
            axis=1,
        )
        part = jnp.dot(wide, turned[p], preferred_element_type=jnp.float32)
        if p == 0:
            acc[...] = part
            return
        if p < pieces - 1:
            acc[...] += part
            return
        part = (part + acc[...]) * (1.0 / float(all_terms) ** 0.5)
        for s in range(2):
            block = jnp.where(furthest < dims[s], part[s * rows : (s + 1) * rows], 0.0)
            (first_out, second_out)[h][s] = block
            if h == 0:
                for i, (q, r) in enumerate(chunks):
                    own[1, i, s] = block[
                        r * height : (r + 1) * height, q * LANES : (q + 1) * LANES
                    ].astype(jnp.bfloat16)

    def finish_piece(h, p):
        for r in range(HALVES):
            for k in range(1, n_col):
                z_copy(h, p * HALVES + r, k, lax.rem(c + n_col - k, n_col)).wait_recv()
        product(h, p)

    def settle_env():
        load_left.wait()
        load_right.wait()
        for k in range(1, n_col):
            for copy in env_copies(k, lax.rem(c + n_col - k, n_col), c):
                copy.wait_recv()
        for p in range(pieces):
            for w in range(all_terms):
                turned[p, w * LANES : (w + 1) * LANES, :] = right[
                    w, :, p * LANES : (p + 1) * LANES
                ].T

    def apply(h, theta_of, lag):
        theta = None
        count = len(chunks)
        for i in range(count + lag + 1):
            if i < count:
                to_pair(h, i).wait_recv()

                @pl.when(has_onward)
                def _():
                    to_onward(h, i).start()

                if i == 0:

                    @pl.when(jnp.logical_not(first_core))
                    def _():
                        for m in range(1, count):
                            to_pair(h, m).start()

                    if h == 0:
                        pl.when(first_core)(start_env)

                combine_near(h, i)
                if h == 0 and i == 2 * HALVES:
                    settle_env()

            j = i - lag
            if 0 <= j < count:

                @pl.when(has_source)
                def _():
                    to_onward(h, j).wait_recv()

                if j == 0 and theta_of is not None:
                    theta = theta_of()
                combine(h, j, theta)
                for k in range(1, n_col):
                    z_copy(h, j, k, c).start()
            j = i - lag - 1
            if j >= 0 and j % HALVES == HALVES - 1:
                if h == 1 and j == count - 1:
                    settle_sends()
                finish_piece(h, j // HALVES)

    def settle(ref, sem):
        pltpu.make_async_copy(ref, ref, sem).wait()

    def inner_product(with_sigma):
        total = None
        for i, (p, r) in enumerate(chunks):
            for s in range(2):
                v = own[0, i, s].astype(jnp.float32)
                w = v
                if with_sigma:
                    w = first_out[
                        s, r * height : (r + 1) * height, p * LANES : (p + 1) * LANES
                    ]
                term = jnp.sum((v * w).reshape(height // 8, 8, LANES), axis=0)
                total = term if total is None else total + term
        return total

    stat_own[1] = inner_product(False)
    apply(0, None, 1)
    stat_own[0] = inner_product(True)

    def stat_to_mate(m):
        return pltpu.make_async_remote_copy(
            src_ref=stat_own,
            dst_ref=stat_mate.at[m - 1],
            send_sem=stat_sem.at[0],
            recv_sem=stat_sem.at[1],
            device_id=mate(m),
            device_id_type=MESH,
        )

    def stat_to_other(m):
        return pltpu.make_async_remote_copy(
            src_ref=stat_sum,
            dst_ref=stat_far.at[m - 1],
            send_sem=stat_sem.at[2],
            recv_sem=stat_sem.at[3],
            device_id=other(m),
            device_id_type=MESH,
        )

    for m in range(1, mates):
        stat_to_mate(m).start()
    start_halo(1)
    settle(stat_mate, stat_sem.at[1])
    stat_sum[...] = stat_own[...] + jnp.sum(stat_mate[...], axis=0)

    @pl.loop(1, others)
    def _(m):
        stat_to_other(m).start()

    def theta_of():
        settle(stat_far, stat_sem.at[3])
        total = stat_sum[...] + jnp.sum(stat_far[...], axis=0)
        sums = [jnp.sum(total[q], axis=(0, 1), keepdims=True) for q in range(2)]
        return sums[0] / sums[1]

    def settle_sends():
        settle(stat_mate, stat_sem.at[0])
        settle(stat_far, stat_sem.at[2])
        settle(own, near_send)

        @pl.when(has_onward)
        def _():
            settle(near, far_send)

        for k in range(1, n_col):
            for copy in env_copies(k, c, lax.rem(c + k, n_col)):
                copy.wait_send()

    apply(1, theta_of, 2)
    for k in range(1, n_col):
        settle(own, z_send.at[k - 1])


def body(n_blk, n_col, psi, dims, pattern, left_env, right_env):
    sectors, rows, width = psi.shape
    terms = left_env.shape[1] * n_col
    chunks = (width // LANES) * HALVES
    halo = (chunks, sectors, rows // HALVES, LANES)
    bf16, f32 = jnp.bfloat16, jnp.float32
    dma = pltpu.SemaphoreType.DMA
    vmem = pltpu.VMEM
    hbm = pl.BlockSpec(memory_space=pl.ANY)
    out = vmem(psi.shape, f32)
    return pl.pallas_call(
        functools.partial(kernel, n_blk, n_col),
        out_shape=(out, out),
        in_specs=[hbm] * 5,
        out_specs=(pl.BlockSpec(memory_space=vmem),) * 2,
        scratch_shapes=[
            pltpu.SMEM(dims.shape, jnp.int32),
            pltpu.SMEM(pattern.shape, jnp.int32),
            vmem((sectors, rows, width), bf16),
            vmem((2, *halo), bf16),
            vmem((2, *halo), bf16),
            vmem((2, *halo), bf16),
            vmem((2, width // LANES, sectors, width, LANES), bf16),
            vmem(halo, f32),
            vmem(halo, f32),
            vmem((sectors, terms, rows, width), bf16),
            vmem((terms, width, width), bf16),
            vmem((width // LANES, terms * LANES, width), bf16),
            vmem((sectors * rows, width), f32),
            vmem((2, 8, LANES), f32),
            vmem((2 * n_col - 1, 2, 8, LANES), f32),
            vmem((2, 8, LANES), f32),
            vmem((n_blk // 2 - 1, 2, 8, LANES), f32),
            dma((5,)),
            dma(()),
            dma((2, chunks)),
            dma(()),
            dma((2, chunks)),
            dma((n_col - 1,)),
            dma((2, n_col - 1, chunks)),
            dma((n_col - 1, 2)),
            dma((n_col - 1, 2)),
            dma((4,)),
        ],
        compiler_params=pltpu.CompilerParams(
            collective_id=0, has_side_effects=True, vmem_limit_bytes=60 * 1024 * 1024
        ),
    )(dims, pattern, psi, left_env, right_env)


def solution(mesh):
    return jax.shard_map(
        functools.partial(body, mesh.shape["blk"], mesh.shape["col"]),
        mesh=mesh,
        in_specs=(
            P("blk", "col", None),
            P("blk"),
            P("blk", None),
            P("blk", "col", None, None),
            P("col", None, None),
        ),
        out_specs=(P("blk", "col", None), P("blk", "col", None)),
        check_vma=False,
    )
```

```python
import functools

import jax
import jax.numpy as jnp
from jax import lax
from jax.experimental import pallas as pl
from jax.experimental.pallas import tpu as pltpu
from jax.sharding import PartitionSpec as P

MESH = pl.DeviceIdType.MESH
LANES = 128
HALVES = 1


def kernel(
    n_blk,
    n_col,
    dims_in,
    pattern_in,
    psi,
    left_env,
    right_env,
    first_out,
    second_out,
    dims,
    pattern,
    raw,
    own,
    near,
    far,
    z,
    z_psi,
    early,
    left,
    right,
    turned,
    acc,
    stat_own,
    stat_mate,
    stat_sum,
    stat_far,
    local_sem,
    near_send,
    near_recv,
    far_send,
    far_recv,
    z_send,
    z_recv,
    env_send,
    env_recv,
    stat_sem,
):
    b = lax.axis_index("blk")
    c = lax.axis_index("col")
    sectors, rows, width = psi.shape
    terms = left_env.shape[1]
    all_terms = terms * n_col
    pieces = width // LANES
    height = rows // HALVES
    chunks = [(p, r) for p in range(pieces) for r in range(HALVES)]
    even = lax.rem(b, 2) == 0
    pair = b + 1 - 2 * lax.rem(b, 2)
    onward = b + 2 - 4 * lax.rem(b, 2)
    source = b - 2 + 4 * lax.rem(b, 2)
    has_onward = (onward >= 0) & (onward < n_blk)
    has_source = (source >= 0) & (source < n_blk)
    my_rows = pl.ds(pl.multiple_of(c * rows, 16), rows)

    load_psi = pltpu.make_async_copy(psi, raw, local_sem.at[0])
    load_psi.start()
    load_dims = pltpu.make_async_copy(dims_in, dims, local_sem.at[3])
    load_dims.start()
    load_pattern = pltpu.make_async_copy(pattern_in, pattern, local_sem.at[4])
    load_pattern.start()
    load_left = pltpu.make_async_copy(
        left_env.at[:, :, my_rows, :], left.at[:, pl.ds(c * terms, terms)], local_sem.at[1]
    )
    load_left.start()
    load_right = pltpu.make_async_copy(
        right_env, right.at[pl.ds(c * terms, terms)], local_sem.at[2]
    )
    load_right.start()

    barrier = pltpu.get_barrier_semaphore()

    side = lax.rem(b, 2)
    mates, others = 2 * n_col, n_blk // 2

    def mate(m):
        f = lax.rem(side * n_col + c + m, mates)
        return (b - side + f // n_col, lax.rem(f, n_col))

    def other(m):
        return (lax.rem(b + 2 * m, n_blk), c)

    @pl.loop(1, others)
    def _(m):
        pl.semaphore_signal(barrier, inc=1, device_id=other(m), device_id_type=MESH)

    for m in range(1, mates):
        pl.semaphore_signal(barrier, inc=1, device_id=mate(m), device_id_type=MESH)

    load_dims.wait()
    load_pattern.wait()
    load_psi.wait()
    row_ids = c * rows + lax.broadcasted_iota(jnp.int32, (rows, width), 0)
    col_ids = lax.broadcasted_iota(jnp.int32, (rows, width), 1)
    furthest = jnp.maximum(row_ids, col_ids)
    for s in range(sectors):
        masked_psi = jnp.where(furthest < dims[s], raw[s].astype(jnp.float32), 0.0)
        for i, (p, r) in enumerate(chunks):
            own[0, i, s] = masked_psi[
                r * height : (r + 1) * height, p * LANES : (p + 1) * LANES
            ].astype(jnp.bfloat16)

    @pl.when(jnp.logical_not(has_source))
    def _():
        far[...] = jnp.zeros_like(far)

    pl.semaphore_wait(barrier, mates + others - 2)

    def to_pair(h, i):
        return pltpu.make_async_remote_copy(
            src_ref=own.at[h, i],
            dst_ref=near.at[h, i],
            send_sem=near_send,
            recv_sem=near_recv.at[h, i],
            device_id=(pair, c),
            device_id_type=MESH,
        )

    def to_onward(h, i):
        return pltpu.make_async_remote_copy(
            src_ref=near.at[h, i],
            dst_ref=far.at[h, i],
            send_sem=far_send,
            recv_sem=far_recv.at[h, i],
            device_id=(onward, c),
            device_id_type=MESH,
        )

    first_core = lax.rem(c, 2) == 0

    def start_halo(h):
        to_pair(h, 0).start()

        @pl.when(first_core)
        def _():
            to_pair(h, 1).start()

    def z_part(h, i, holder):
        p, r = chunks[i]
        start = pl.multiple_of(holder * rows + r * height, 16)
        return z.at[h, p, :, pl.ds(start, height), :]

    def z_copy(h, i, k, holder):
        return pltpu.make_async_remote_copy(
            src_ref=z_part(h, i, holder),
            dst_ref=z_part(h, i, holder),
            send_sem=z_send.at[k - 1],
            recv_sem=z_recv.at[h, k - 1, i],
            device_id=(b, lax.rem(c + k, n_col)),
            device_id_type=MESH,
        )

    def env_copies(k, holder, taker):
        took = pl.ds(pl.multiple_of(taker * rows, 16), rows)
        slot = pl.ds(holder * terms, terms)
        return [
            pltpu.make_async_remote_copy(
                src_ref=src,
                dst_ref=dst,
                send_sem=env_send.at[k - 1, j],
                recv_sem=env_recv.at[k - 1, j],
                device_id=(b, lax.rem(c + k, n_col)),
                device_id_type=MESH,
            )
            for j, (src, dst) in enumerate(
                [
                    (left_env.at[:, :, took, :], left.at[:, slot]),
                    (right_env, right.at[slot]),
                ]
            )
        ]

    start_halo(0)

    def start_env():
        for k in range(1, n_col):
            for copy in env_copies(k, c, lax.rem(c + k, n_col)):
                copy.start()

    pl.when(jnp.logical_not(first_core))(start_env)

    coeff = [[pattern[s, j].astype(jnp.float32) for j in range(5)] for s in range(2)]
    zero = jnp.float32(0.0)
    below = ((coeff[0][0], coeff[0][1]), (zero, coeff[1][0]))
    above = ((coeff[0][4], zero), (coeff[1][3], coeff[1][4]))
    inner = ((coeff[0][2], coeff[0][3]), (coeff[1][1], coeff[1][2]))
    near_c = [[jnp.where(even, above[s][k], below[s][k]) for k in range(2)] for s in range(2)]
    far_c = [[jnp.where(even, below[s][k], above[s][k]) for k in range(2)] for s in range(2)]

    def weigh(h, i, parts, total):
        for ref, weights in parts:
            for k in range(2):
                block = ref[h, i, k].astype(jnp.float32)
                for s in range(2):
                    term = weights[s][k] * block
                    total[s] = term if total[s] is None else total[s] + term
        return total

    def combine_near(h, i):
        total = weigh(h, i, ((own, inner), (near, near_c)), [None, None])
        for s in range(2):
            if h == 1:
                early[i, s] = total[s]
            else:
                z_psi[i, s] = total[s]

    def combine(h, i, theta):
        p, r = chunks[i]
        start = pl.multiple_of(c * rows + r * height, 16)
        ref = early if h == 1 else z_psi
        total = weigh(h, i, ((far, far_c),), [ref[i, s] for s in range(2)])
        for s in range(2):
            if h == 0:
                z_psi[i, s] = total[s]
            else:
                total[s] = total[s] - theta * z_psi[i, s]
            z[h, p, s, pl.ds(start, height), :] = total[s].astype(jnp.bfloat16)

    def product(h, p):
        temp = []
        for s in range(2):
            t = jnp.dot(
                left[s].reshape(all_terms * rows, width),
                z[h, p, s],
                preferred_element_type=jnp.float32,
            ).astype(jnp.bfloat16)
            temp.append(t)
        wide = jnp.concatenate(
            [
                jnp.concatenate([t[w * rows : (w + 1) * rows] for t in temp], axis=0)
                for w in range(all_terms)
            ],
            axis=1,
        )
        part = jnp.dot(wide, turned[p], preferred_element_type=jnp.float32)
        if p == 0:
            acc[...] = part
            return
        if p < pieces - 1:
            acc[...] += part
            return
        part = (part + acc[...]) * (1.0 / float(all_terms) ** 0.5)
        for s in range(2):
            block = jnp.where(furthest < dims[s], part[s * rows : (s + 1) * rows], 0.0)
            (first_out, second_out)[h][s] = block
            if h == 0:
                for i, (q, r) in enumerate(chunks):
                    own[1, i, s] = block[
                        r * height : (r + 1) * height, q * LANES : (q + 1) * LANES
                    ].astype(jnp.bfloat16)

    def finish_piece(h, p):
        for r in range(HALVES):
            for k in range(1, n_col):
                z_copy(h, p * HALVES + r, k, lax.rem(c + n_col - k, n_col)).wait_recv()
        product(h, p)

    def settle_env():
        load_left.wait()
        load_right.wait()
        for k in range(1, n_col):
            for copy in env_copies(k, lax.rem(c + n_col - k, n_col), c):
                copy.wait_recv()
        for p in range(pieces):
            for w in range(all_terms):
                turned[p, w * LANES : (w + 1) * LANES, :] = right[
                    w, :, p * LANES : (p + 1) * LANES
                ].T

    def apply(h, theta_of, lag):
        theta = None
        count = len(chunks)
        for i in range(count + lag + 1):
            if i < count:
                to_pair(h, i).wait_recv()

                @pl.when(has_onward)
                def _():
                    to_onward(h, i).start()

                for core_is, ahead in ((first_core, 2), (jnp.logical_not(first_core), 1)):
                    if i + ahead < count:
                        pl.when(core_is)(to_pair(h, i + ahead).start)
                if i == 0 and h == 0:
                    pl.when(first_core)(start_env)

                combine_near(h, i)
                if h == 0 and i == 2 * HALVES:
                    settle_env()

            j = i - lag
            if 0 <= j < count:

                @pl.when(has_source)
                def _():
                    to_onward(h, j).wait_recv()

                if j == 0 and theta_of is not None:
                    theta = theta_of()
                combine(h, j, theta)
                for k in range(1, n_col):
                    z_copy(h, j, k, c).start()
            j = i - lag - 1
            if j >= 0 and j % HALVES == HALVES - 1:
                if h == 1 and j == count - 1:
                    settle_sends()
                finish_piece(h, j // HALVES)

    def settle(ref, sem):
        pltpu.make_async_copy(ref, ref, sem).wait()

    def inner_product(with_sigma):
        total = None
        for i, (p, r) in enumerate(chunks):
            for s in range(2):
                v = own[0, i, s].astype(jnp.float32)
                w = v
                if with_sigma:
                    w = first_out[
                        s, r * height : (r + 1) * height, p * LANES : (p + 1) * LANES
                    ]
                term = jnp.sum((v * w).reshape(height // 8, 8, LANES), axis=0)
                total = term if total is None else total + term
        return total

    stat_own[1] = inner_product(False)
    apply(0, None, 1)
    stat_own[0] = inner_product(True)

    def stat_to_mate(m):
        return pltpu.make_async_remote_copy(
            src_ref=stat_own,
            dst_ref=stat_mate.at[m - 1],
            send_sem=stat_sem.at[0],
            recv_sem=stat_sem.at[1],
            device_id=mate(m),
            device_id_type=MESH,
        )

    def stat_to_other(m):
        return pltpu.make_async_remote_copy(
            src_ref=stat_sum,
            dst_ref=stat_far.at[m - 1],
            send_sem=stat_sem.at[2],
            recv_sem=stat_sem.at[3],
            device_id=other(m),
            device_id_type=MESH,
        )

    for m in range(1, mates):
        stat_to_mate(m).start()
    start_halo(1)
    settle(stat_mate, stat_sem.at[1])
    stat_sum[...] = stat_own[...] + jnp.sum(stat_mate[...], axis=0)

    @pl.loop(1, others)
    def _(m):
        stat_to_other(m).start()

    def theta_of():
        settle(stat_far, stat_sem.at[3])
        total = stat_sum[...] + jnp.sum(stat_far[...], axis=0)
        sums = [jnp.sum(total[q], axis=(0, 1), keepdims=True) for q in range(2)]
        return sums[0] / sums[1]

    def settle_sends():
        settle(stat_mate, stat_sem.at[0])
        settle(stat_far, stat_sem.at[2])
        settle(own, near_send)

        @pl.when(has_onward)
        def _():
            settle(near, far_send)

        for k in range(1, n_col):
            for copy in env_copies(k, c, lax.rem(c + k, n_col)):
                copy.wait_send()

    apply(1, theta_of, 2)
    for k in range(1, n_col):
        settle(own, z_send.at[k - 1])


def body(n_blk, n_col, psi, dims, pattern, left_env, right_env):
    sectors, rows, width = psi.shape
    terms = left_env.shape[1] * n_col
    chunks = (width // LANES) * HALVES
    halo = (chunks, sectors, rows // HALVES, LANES)
    bf16, f32 = jnp.bfloat16, jnp.float32
    dma = pltpu.SemaphoreType.DMA
    vmem = pltpu.VMEM
    hbm = pl.BlockSpec(memory_space=pl.ANY)
    out = vmem(psi.shape, f32)
    return pl.pallas_call(
        functools.partial(kernel, n_blk, n_col),
        out_shape=(out, out),
        in_specs=[hbm] * 5,
        out_specs=(pl.BlockSpec(memory_space=vmem),) * 2,
        scratch_shapes=[
            pltpu.SMEM(dims.shape, jnp.int32),
            pltpu.SMEM(pattern.shape, jnp.int32),
            vmem((sectors, rows, width), bf16),
            vmem((2, *halo), bf16),
            vmem((2, *halo), bf16),
            vmem((2, *halo), bf16),
            vmem((2, width // LANES, sectors, width, LANES), bf16),
            vmem(halo, f32),
            vmem(halo, f32),
            vmem((sectors, terms, rows, width), bf16),
            vmem((terms, width, width), bf16),
            vmem((width // LANES, terms * LANES, width), bf16),
            vmem((sectors * rows, width), f32),
            vmem((2, 8, LANES), f32),
            vmem((2 * n_col - 1, 2, 8, LANES), f32),
            vmem((2, 8, LANES), f32),
            vmem((n_blk // 2 - 1, 2, 8, LANES), f32),
            dma((5,)),
            dma(()),
            dma((2, chunks)),
            dma(()),
            dma((2, chunks)),
            dma((n_col - 1,)),
            dma((2, n_col - 1, chunks)),
            dma((n_col - 1, 2)),
            dma((n_col - 1, 2)),
            dma((4,)),
        ],
        compiler_params=pltpu.CompilerParams(
            collective_id=0, has_side_effects=True, vmem_limit_bytes=60 * 1024 * 1024
        ),
    )(dims, pattern, psi, left_env, right_env)


def solution(mesh):
    return jax.shard_map(
        functools.partial(body, mesh.shape["blk"], mesh.shape["col"]),
        mesh=mesh,
        in_specs=(
            P("blk", "col", None),
            P("blk"),
            P("blk", None),
            P("blk", "col", None, None),
            P("col", None, None),
        ),
        out_specs=(P("blk", "col", None), P("blk", "col", None)),
        check_vma=False,
    )
```
